32 devices in a mesh: grp: 8 (over y, x, core), tp: 4 (over z).
Axes of the slice: x: 2, y: 2, z: 4, core: 2. Of those that a mesh axis runs over, the one named last changes fastest.
Arguments:
- queries: bfloat16 [32, 2, 4096], P('grp'), may hold values from -8 to 8
- cache_keys: bfloat16 [32, 512, 512], P('grp', 'tp'), may hold values from -8 to 8
- cache_values: bfloat16 [32, 512, 512], P('grp', 'tp'), may hold values from -6 to 6
- new_keys: bfloat16 [32, 2, 512], P('grp'), may hold values from -6 to 6
- new_values: bfloat16 [32, 2, 512], P('grp'), may hold values from -6 to 6
- lengths: int32 [32], P('grp'), may hold values from 2 to 512
- residual: bfloat16 [32, 2, 4096], P('grp'), may hold values from -0.1796875 to 0.1796875
- norm_gain: float32 [4096], replicated, may hold values from 0.25 to 1.75
- w_gate: float32 [4096, 2400], P('grp', 'tp'), may hold values from -0.09375 to 0.09375
- w_down: float32 [4096, 2400], P('grp', 'tp'), may hold values from -0.125 to 0.125
Outputs:
- mixed: bfloat16 [32, 2, 4096], P('grp')
The draws below stay inside these ranges and needn't reach their ends.
All inputs are finite; a program needn't handle non-finite values.
Results may differ from the reference program's by a relative error of at most 0.028.
Values may be sent and summed in bfloat16 or wider, within the bound.
A program may use at most 64 MiB of HBM per device.

```python
import jax
import jax.numpy as jnp
from jax import lax

HD = 128
HQ = 32
KVH = 4
STEPS = 2
D = 4096
FF = 2400
ROWS_ALL = 32
CTX = 512


def draw_queries(key, part):
    values = jax.random.truncated_normal(jax.random.fold_in(key, 11), -6.0, 6.0, (ROWS_ALL, STEPS, HQ * HD), jnp.float32)
    return values.astype(jnp.bfloat16)


def draw_cache_keys(key, part):
    values = jax.random.truncated_normal(jax.random.fold_in(key, 12), -6.0, 6.0, (ROWS_ALL, CTX, KVH * HD), jnp.float32)
    return values.astype(jnp.bfloat16)


def place_ends(drawn, rng, smallest, largest):
    spot = [jax.random.randint(jax.random.fold_in(rng, axis), (), 0, length) for axis, length in enumerate(drawn.shape)]
    main_axis = drawn.shape.index(max(drawn.shape))
    neighbour = spot[:main_axis] + [(spot[main_axis] + 1) % drawn.shape[main_axis]] + spot[main_axis + 1:]
    return drawn.at[tuple(spot)].set(smallest).at[tuple(neighbour)].set(largest)


def block_levels(key, shape, shards, low, largest):
    def one(axis_at, blocks):
        draws = jax.random.uniform(jax.random.fold_in(jax.random.fold_in(key, 6), axis_at), (blocks,), jnp.float32, low / len(shards), largest / len(shards))
        return jnp.repeat(jnp.exp(draws), shape[axis_at] // blocks).reshape((-1,) + (1,) * (len(shape) - axis_at - 1))

    gain = one(*shards[0])
    for cut in shards[1:]:
        gain = gain * one(*cut)
    return gain


def gaussian(key, extent, spread, limit, shards=(), kind=jnp.bfloat16):
    values = jax.random.normal(key, extent, jnp.float32) * spread
    if len(shards) > 0:
        values = block_levels(key, extent, shards, -0.22, 0.18) * values
    return jnp.clip(values, min=-limit, max=limit).astype(kind)


def setup_inputs(seed: int = 0) -> dict:
    streams_of = jax.random.split(jax.random.key(seed), 11)
    queries = draw_queries(jax.random.fold_in(streams_of[10], 71), 0)
    cache_keys = draw_cache_keys(jax.random.fold_in(streams_of[10], 71), 0)
    cache_values = gaussian(streams_of[2], (ROWS_ALL, CTX, KVH * HD), 1.0, 6.0, ((0, 8), (1, 4)))
    new_keys = gaussian(streams_of[3], (ROWS_ALL, STEPS, KVH * HD), 1.0, 6.0, ((0, 8),))
    new_values = gaussian(streams_of[4], (ROWS_ALL, STEPS, KVH * HD), 1.0, 6.0, ((0, 8),))
    lengths = place_ends(jax.random.randint(streams_of[5], (ROWS_ALL,), 2, CTX + 1), jax.random.fold_in(streams_of[5], 1), 2, CTX).astype(jnp.int32)
    residual = gaussian(streams_of[6], (ROWS_ALL, STEPS, D), 0.03, 0.1796875, ((0, 8),))
    norm_gain = jnp.clip(1.0 + 0.15 * jax.random.normal(streams_of[7], (D,), jnp.float32), 0.25, 1.75)
    w_gate = gaussian(streams_of[8], (D, FF), D ** -0.5, 0.09375, ((0, 8), (1, 4)), jnp.float32)
    w_down = gaussian(streams_of[9], (D, FF), FF ** -0.5, 0.125, ((0, 8), (1, 4)), jnp.float32)
    return {"queries": queries, "cache_keys": cache_keys, "cache_values": cache_values, "new_keys": new_keys, "new_values": new_values, "lengths": lengths, "residual": residual, "norm_gain": norm_gain, "w_gate": w_gate, "w_down": w_down}


masked_score = -1e+30

def reference(queries, cache_keys, cache_values, new_keys, new_values, lengths, residual, norm_gain, w_gate, w_down):
    per_group = HQ // KVH
    inv_root = HD ** (-0.5)
    causal = jnp.arange(STEPS, dtype=jnp.int32)[:, None] >= jnp.arange(STEPS, dtype=jnp.int32)[None, :]
    causal = causal[:, None, None, :]

    def one_row(item):
        query_row, key_rows, value_rows, fresh_keys, fresh_values, length = item
        query_heads = query_row.astype(jnp.float32).reshape(STEPS, KVH, per_group, HD)
        key_heads = key_rows.astype(jnp.float32).reshape(CTX, KVH, HD)
        value_heads = value_rows.astype(jnp.float32).reshape(CTX, KVH, HD)
        fresh_key_heads = fresh_keys.astype(jnp.float32).reshape(STEPS, KVH, HD)
        fresh_value_heads = fresh_values.astype(jnp.float32).reshape(STEPS, KVH, HD)
        visible = jnp.arange(CTX, dtype=jnp.int32) < length
        cached_scores = jnp.einsum('sjgd,cjd->sjgc', query_heads, key_heads) * inv_root
        cached_scores = jnp.where(visible, cached_scores, masked_score)
        fresh_scores = jnp.einsum('sjgd,tjd->sjgt', query_heads, fresh_key_heads) * inv_root
        fresh_scores = jnp.where(causal, fresh_scores, masked_score)
        highest = jnp.maximum(lax.optimization_barrier(jnp.max(cached_scores, axis=-1)), lax.optimization_barrier(jnp.max(fresh_scores, axis=-1)))
        cached_weights = jnp.where(visible, jnp.exp(cached_scores - highest[..., None]), 0.0)
        fresh_weights = jnp.where(causal, jnp.exp(fresh_scores - highest[..., None]), 0.0)
        totals = lax.optimization_barrier(jnp.sum(cached_weights, axis=-1)) + lax.optimization_barrier(jnp.sum(fresh_weights, axis=-1))
        accum = jnp.einsum('sjgc,cjd->sjgd', cached_weights.astype(jnp.bfloat16).astype(jnp.float32), value_heads)
        accum = accum + jnp.einsum('sjgt,tjd->sjgd', fresh_weights.astype(jnp.bfloat16).astype(jnp.float32), fresh_value_heads)
        return (accum / totals[..., None]).reshape(STEPS, HQ * HD)
    context = lax.map(one_row, (queries, cache_keys, cache_values, new_keys, new_values, lengths))
    summed = residual.astype(jnp.float32) + context
    mean_square = lax.optimization_barrier(jnp.mean(summed * summed, axis=-1, keepdims=True))
    normed = (summed * lax.rsqrt(mean_square + 1e-05) * norm_gain.astype(jnp.float32)).astype(jnp.bfloat16)
    flat = normed.reshape(ROWS_ALL * STEPS, D)
    gate = jnp.dot(flat, w_gate.astype(jnp.bfloat16), preferred_element_type=jnp.float32)
    hidden = jax.nn.silu(gate).astype(jnp.bfloat16)
    mlp = lax.dot_general(hidden, w_down.astype(jnp.bfloat16), (((1,), (1,)), ((), ())), preferred_element_type=jnp.float32)
    return (summed + mlp.reshape(ROWS_ALL, STEPS, D)).astype(jnp.bfloat16)
```

```python
import functools

import jax
import jax.numpy as jnp
from jax import lax
from jax.experimental import pallas as pl
from jax.experimental.pallas import tpu as pltpu
from jax.sharding import PartitionSpec as P

HD = 128
KVH = 4


masked_score = -1e30


def merged_2(shard, axis, join):
    gathered = jax.tree.map(
        lambda a, kind: lax.all_gather(a.astype(kind), axis),
        shard,
        jax.tree.map(lambda a: jnp.bfloat16 if a.dtype == jnp.float32 else a.dtype, shard),
    )

    def take(source):
        return jax.tree.map(
            lambda a, own: lax.dynamic_index_in_dim(a, source, 0, False).astype(own.dtype),
            gathered,
            shard,
        )

    return lax.fori_loop(
        1, lax.axis_size(axis), lambda source, state: join(state, take(source)), take(0)
    )


def combine_parts(earlier, later):
    first_max, first_total, first_accum = earlier
    second_max, second_total, second_accum = later
    joint_max = jnp.maximum(first_max, second_max)
    first_factor = jnp.exp(first_max - joint_max)
    second_factor = jnp.exp(second_max - joint_max)
    joint_total = first_total * first_factor + second_total * second_factor
    joint_accum = first_accum * first_factor[..., None] + second_accum * second_factor[..., None]
    return (joint_max, joint_total, joint_accum)


def partial_softmax(scores, visible, value_heads, formula):
    scores = jnp.where(visible, scores, masked_score)
    highest = jnp.max(scores, axis=-1)
    weights = jnp.where(visible, jnp.exp(scores - highest[..., None]), 0.0)
    totals = jnp.sum(weights, axis=-1)
    accum = jnp.einsum(
        formula, weights.astype(jnp.bfloat16), value_heads, preferred_element_type=jnp.float32
    )
    return (highest, totals, accum)


def gathered_weights(
    queries,
    cache_keys,
    cache_values,
    new_keys,
    new_values,
    lengths,
    residual,
    norm_gain,
    w_gate,
    w_down,
):
    row_count, step_count, features = queries.shape
    positions = cache_keys.shape[1]
    per_group = features // (KVH * HD)
    inv_root = HD ** (-0.5)
    query_heads = queries.reshape(row_count, step_count, KVH, per_group, HD)
    key_heads = cache_keys.reshape(row_count, positions, KVH, HD)
    value_heads = cache_values.reshape(row_count, positions, KVH, HD)
    cached_scores = (
        jnp.einsum("rsjgd,rcjd->rsjgc", query_heads, key_heads, preferred_element_type=jnp.float32)
        * inv_root
    )
    offset = lax.axis_index("tp") * positions
    places = offset + lax.broadcasted_iota(jnp.int32, (row_count, positions), 1)
    visible = (places < lengths[:, None])[:, None, None, None, :]
    local_part = partial_softmax(cached_scores, visible, value_heads, "rsjgc,rcjd->rsjgd")
    merged = merged_2(local_part, "tp", combine_parts)
    fresh_key_heads = new_keys.reshape(row_count, step_count, KVH, HD)
    fresh_value_heads = new_values.reshape(row_count, step_count, KVH, HD)
    fresh_scores = (
        jnp.einsum(
            "rsjgd,rtjd->rsjgt", query_heads, fresh_key_heads, preferred_element_type=jnp.float32
        )
        * inv_root
    )
    causal = lax.broadcasted_iota(jnp.int32, (step_count, step_count), 0) >= lax.broadcasted_iota(
        jnp.int32, (step_count, step_count), 1
    )
    causal = causal[None, :, None, None, :]
    fresh_part = partial_softmax(fresh_scores, causal, fresh_value_heads, "rsjgt,rtjd->rsjgd")
    joint_max, joint_total, joint_accum = combine_parts(merged, fresh_part)
    context = (joint_accum / joint_total[..., None]).reshape(row_count, step_count, features)
    summed = residual.astype(jnp.float32) + context
    mean_square = jnp.mean(summed * summed, axis=-1, keepdims=True)
    normed = (summed * lax.rsqrt(mean_square + 1e-05) * norm_gain).astype(jnp.bfloat16)
    flat = normed.reshape(row_count * step_count, features)
    gate_policy, down_policy = (
        lax.all_gather(w_gate.astype(jnp.bfloat16), "grp", axis=0, tiled=True),
        lax.all_gather(w_down.astype(jnp.bfloat16), "grp", axis=0, tiled=True),
    )
    gate = jnp.dot(flat, gate_policy, preferred_element_type=jnp.float32)
    hidden = jax.nn.silu(gate).astype(jnp.bfloat16)
    partial_sum = lax.dot_general(
        hidden, down_policy, (((1,), (1,)), ((), ())), preferred_element_type=jnp.float32
    )
    mlp = lax.psum(partial_sum.astype(jnp.bfloat16), "tp").astype(jnp.float32)
    return (summed + mlp.reshape(row_count, step_count, features)).astype(jnp.bfloat16)


MESH = pl.DeviceIdType.MESH
BF16, F32 = jnp.bfloat16, jnp.float32


def layer_kernel(
    n_g,
    n_t,
    lengths_ref,
    q_ref,
    nk_ref,
    nv_ref,
    res_ref,
    gain_ref,
    ck_hbm,
    cv_hbm,
    wg_hbm,
    wd_hbm,
    mlp_ref,
    sum_ref,
    ck,
    cv,
    wg32,
    wd32,
    wg,
    wd,
    send_o,
    recv_o,
    send_l,
    recv_l,
    send_x,
    recv_x,
    x_rows,
    send_g,
    recv_g,
    send_h,
    recv_h,
    send_m,
    recv_m,
    m_rows,
    send_f,
    load_sem,
    w_sem,
    o_send_sem,
    o_recv_sem,
    l_send_sem,
    l_recv_sem,
    c_send_sem,
    c_recv_sem,
    x_send_sem,
    x_recv_sem,
    g_send_sem,
    g_recv_sem,
    h_send_sem,
    h_recv_sem,
    m_send_sem,
    m_recv_sem,
    f_send_sem,
    f_recv_sem,
):
    g, t = lax.axis_index("grp"), lax.axis_index("tp")
    n = n_g * n_t
    rows, positions = ck.shape[0], ck.shape[1]
    steps = nk_ref.shape[1]
    heads = gain_ref.shape[0]
    per_key = heads // KVH
    per_col = heads // n_g
    inv_root = HD ** (-0.5)

    def peer(k):
        return lax.rem(g + k // n_t, n_g), lax.rem(t + lax.rem(k, n_t), n_t)

    def cache_copy(r, which):
        source, target = ((ck_hbm, ck), (cv_hbm, cv))[which]
        return pltpu.make_async_copy(source.at[r], target.at[r], load_sem.at[which, r])

    order = [lax.rem(t + k, n_t) for k in (*range(1, n_t), 0)]
    for r in order:
        cache_copy(r, 0).start()
        cache_copy(r, 1).start()
    load_gate = pltpu.make_async_copy(wg_hbm, wg32, w_sem.at[0])
    load_down = pltpu.make_async_copy(wd_hbm, wd32, w_sem.at[1])
    load_gate.start()
    load_down.start()

    barrier = pltpu.get_barrier_semaphore()

    def greet(k, carry):
        pl.semaphore_signal(barrier, inc=1, device_id=peer(k), device_id_type=MESH)
        return carry

    lax.fori_loop(1, n, greet, 0)

    sub = lax.broadcasted_iota(jnp.int32, (steps * heads, HD), 0)
    lane = lax.broadcasted_iota(jnp.int32, (steps * heads, HD), 1)
    diagonal = sub == lane

    row_copies = []
    for k, r in enumerate(order):
        cache_copy(r, 0).wait()
        cache_copy(r, 1).wait()
        place = t * positions + lax.broadcasted_iota(
            jnp.int32, (steps * per_key, positions), 1
        )
        visible = place < lengths_ref[r]
        query = q_ref[r].astype(F32)
        parts, logs = [], []
        for j in range(KVH):
            own = jnp.concatenate(
                [
                    query[s * heads + j * per_key : s * heads + (j + 1) * per_key]
                    for s in range(steps)
                ],
                axis=0,
            ).astype(BF16)
            keys = ck[r, :, j * HD : (j + 1) * HD]
            values = cv[r, :, j * HD : (j + 1) * HD]
            scores = (
                lax.dot_general(own, keys, (((1,), (1,)), ((), ())), preferred_element_type=F32)
                * inv_root
            )
            scores = jnp.where(visible, scores, masked_score)
            highest = jnp.max(scores, axis=-1, keepdims=True)
            weights = jnp.where(visible, jnp.exp(scores - highest), 0.0)
            total = jnp.sum(weights, axis=-1, keepdims=True)
            accum = jnp.dot(weights.astype(BF16), values, preferred_element_type=F32)
            some = total > 0.0
            safe = jnp.where(some, total, 1.0)
            parts.append(accum / safe)
            logs.append(jnp.where(some, highest + jnp.log(safe), masked_score))

        def by_step(pieces):
            return jnp.concatenate(
                [p[s * per_key : (s + 1) * per_key] for s in range(steps) for p in pieces], axis=0
            )

        mean_values = by_step(parts).astype(BF16)
        log_lanes = jnp.sum(
            jnp.where(diagonal, by_step(logs), 0.0), axis=0, keepdims=True
        )
        log_lanes = jnp.broadcast_to(log_lanes, recv_l.shape[1:])
        if k == n_t - 1:
            recv_o[t] = mean_values
            recv_l[t] = log_lanes
        else:
            send_o[k] = mean_values
            send_l[k] = log_lanes
            if k == 0:
                pl.semaphore_wait(barrier, n - 1)
            for source, target, send_sem, recv_sem in (
                (send_o, recv_o, o_send_sem, o_recv_sem),
                (send_l, recv_l, l_send_sem, l_recv_sem),
            ):
                copy = pltpu.make_async_remote_copy(
                    src_ref=source.at[k],
                    dst_ref=target.at[t],
                    send_sem=send_sem.at[k],
                    recv_sem=recv_sem.at[k],
                    device_id=(g, r),
                    device_id_type=MESH,
                )
                copy.start()
                row_copies.append(copy)

    query = q_ref[t].astype(F32)
    new_keys = nk_ref[t].astype(F32)
    new_values = nv_ref[t].astype(F32)

    def over_heads(tokens, at):
        return jnp.concatenate(
            [
                jnp.broadcast_to(tokens[at : at + 1, j * HD : (j + 1) * HD], (per_key, HD))
                for _ in range(steps)
                for j in range(KVH)
            ],
            axis=0,
        )

    seen = [
        lax.broadcasted_iota(jnp.int32, (steps * heads, 1), 0) >= at * heads for at in range(steps)
    ]
    fresh = [
        jnp.where(
            seen[at],
            jnp.sum(query * over_heads(new_keys, at), axis=-1, keepdims=True) * inv_root,
            masked_score,
        )
        for at in range(steps)
    ]
    load_gate.wait()
    wg[...] = wg32[...].astype(BF16)
    load_down.wait()
    wd[...] = wd32[...].astype(BF16)
    for copy in row_copies:
        copy.wait_recv()

    logs = [
        jnp.sum(jnp.where(diagonal, recv_l[i][0:1], 0.0), axis=-1, keepdims=True)
        for i in range(n_t)
    ]
    joint = functools.reduce(jnp.maximum, logs + fresh)
    total, accum = 0.0, 0.0
    for i in range(n_t):
        weight = jnp.exp(logs[i] - joint)
        total = total + weight
        accum = accum + weight * recv_o[i].astype(F32)
    for at in range(steps):
        weight = jnp.where(seen[at], jnp.exp(fresh[at] - joint), 0.0)
        total = total + weight
        accum = accum + weight.astype(BF16).astype(F32) * over_heads(new_values, at)
    summed = res_ref[t].astype(F32) + accum / total

    normed = []
    for s in range(steps):
        part = summed[s * heads : (s + 1) * heads]
        square = jnp.sum(jnp.sum(part * part, axis=0, keepdims=True), axis=1, keepdims=True)
        normed.append(part * lax.rsqrt(square / (heads * HD) + 1e-05) * gain_ref[...])
    for i in range(n_g):
        send_x[i] = jnp.concatenate(
            [part[i * per_col : (i + 1) * per_col] for part in normed], axis=0
        ).astype(BF16)

    def to_all(source, target, send_sem, recv_sem):
        def one(k):
            to_g, to_t = peer(k)
            return pltpu.make_async_remote_copy(
                src_ref=source.at[to_g],
                dst_ref=target.at[t * n_g + g],
                send_sem=send_sem.at[k - 1],
                recv_sem=recv_sem.at[k - 1],
                device_id=(to_g, to_t),
                device_id_type=MESH,
            )

        return one

    def start_all(one):
        def body(k, carry):
            one(k).start()
            return carry

        lax.fori_loop(1, n, body, 0)

    def wait_all(one, sent):
        def body(k, carry):
            if sent:
                one(k).wait_send()
            else:
                one(k).wait_recv()
            return carry

        lax.fori_loop(1, n, body, 0)

    x_copy = to_all(send_x, recv_x, x_send_sem, x_recv_sem)
    start_all(x_copy)
    recv_x[t * n_g + g] = send_x[g]
    sum_ref[t] = summed.astype(BF16)
    sum_copies = []
    for k in range(1, n_t):
        copy = pltpu.make_async_remote_copy(
            src_ref=sum_ref.at[t],
            dst_ref=sum_ref.at[t],
            send_sem=c_send_sem.at[k - 1],
            recv_sem=c_recv_sem.at[k - 1],
            device_id=(g, lax.rem(t + k, n_t)),
            device_id_type=MESH,
        )
        copy.start()
        sum_copies.append(copy)
    wait_all(x_copy, False)

    height = steps * per_col
    x_rows[...] = recv_x[...].astype(F32).reshape(n * height, HD)
    columns = []
    for c in range(per_col):
        picked = [x_rows[pl.ds(s * per_col + c, n, stride=height), :] for s in range(steps)]
        columns.append(
            jnp.concatenate(
                [p[i * n_g : (i + 1) * n_g] for i in range(n_t) for p in picked], axis=0
            )
        )
    x = jnp.concatenate(columns, axis=1).astype(BF16)
    gate = jnp.dot(x, wg[...], preferred_element_type=F32)
    chunk = send_g.shape[1]
    for i in range(n_g):
        send_g[i] = gate[i * chunk : (i + 1) * chunk].astype(BF16)

    def along_grp(k, source, target, send_sem, recv_sem):
        return pltpu.make_async_remote_copy(
            src_ref=source,
            dst_ref=target.at[g],
            send_sem=send_sem.at[k - 1],
            recv_sem=recv_sem.at[k - 1],
            device_id=(lax.rem(g + k, n_g), t),
            device_id_type=MESH,
        )

    gate_copies = [
        along_grp(k, send_g.at[lax.rem(g + k, n_g)], recv_g, g_send_sem, g_recv_sem)
        for k in range(1, n_g)
    ]
    for copy in gate_copies:
        copy.start()
    recv_g[g] = send_g[g]
    for copy in gate_copies:
        copy.wait_recv()
    whole = functools.reduce(jnp.add, [recv_g[i].astype(F32) for i in range(n_g)])
    mine = (whole / (1.0 + jnp.exp(-whole))).astype(BF16)

    send_h[...] = mine
    hidden_copies = [
        along_grp(k, send_h, recv_h, h_send_sem, h_recv_sem) for k in range(1, n_g)
    ]
    for copy in hidden_copies:
        copy.start()
    recv_h[g] = mine
    for copy in hidden_copies:
        copy.wait_recv()
    hidden = recv_h[...].astype(F32).reshape(n_g * chunk, recv_h.shape[2]).astype(BF16)
    mlp = lax.dot_general(hidden, wd[...], (((1,), (1,)), ((), ())), preferred_element_type=F32)

    part_rows = send_m.shape[1]
    for i in range(n_t):
        send_m[i] = mlp[i * part_rows : (i + 1) * part_rows].astype(BF16)
    mlp_copies = []
    for k in range(1, n_t):
        to_t = lax.rem(t + k, n_t)
        copy = pltpu.make_async_remote_copy(
            src_ref=send_m.at[to_t],
            dst_ref=recv_m.at[t],
            send_sem=m_send_sem.at[k - 1],
            recv_sem=m_recv_sem.at[k - 1],
            device_id=(g, to_t),
            device_id_type=MESH,
        )
        copy.start()
        mlp_copies.append(copy)
    recv_m[t] = send_m[t]
    for copy in mlp_copies:
        copy.wait_recv()
    done = functools.reduce(jnp.add, [recv_m[i].astype(F32) for i in range(n_t)])

    for s in range(steps):
        for c in range(per_col):
            m_rows[pl.ds(s * per_col + c, n_g, stride=height), :] = done[
                s * n_g : (s + 1) * n_g, c * HD : (c + 1) * HD
            ]
    send_f[...] = m_rows[...].reshape(n_g, height, HD).astype(BF16)
    f_copy = to_all(send_f, mlp_ref, f_send_sem, f_recv_sem)
    start_all(f_copy)
    mlp_ref[t * n_g + g] = send_f[g]
    for copy in row_copies + sum_copies + gate_copies + hidden_copies + mlp_copies:
        copy.wait_send()
    wait_all(x_copy, True)
    for copy in sum_copies:
        copy.wait_recv()
    wait_all(f_copy, False)
    wait_all(f_copy, True)


def moved_activations(
    n_g,
    n_t,
    queries,
    cache_keys,
    cache_values,
    new_keys,
    new_values,
    lengths,
    residual,
    norm_gain,
    w_gate,
    w_down,
):
    rows, steps, features = queries.shape
    positions, kv_width = cache_keys.shape[1:]
    depth, units = w_gate.shape
    heads = features // HD
    n = n_g * n_t
    flat = steps * heads
    height = steps * (heads // n_g)
    all_rows = n * steps
    chunk = all_rows // n_g
    part_rows = all_rows // n_t
    vmem = pl.BlockSpec(memory_space=pltpu.VMEM)
    hbm = pl.BlockSpec(memory_space=pl.ANY)
    dma = pltpu.SemaphoreType.DMA
    mlp, summed = pl.pallas_call(
        functools.partial(layer_kernel, n_g, n_t),
        out_shape=(
            jax.ShapeDtypeStruct((n, height, HD), BF16),
            jax.ShapeDtypeStruct((n_t, flat, HD), BF16),
        ),
        in_specs=[pl.BlockSpec(memory_space=pltpu.SMEM)] + [vmem] * 5 + [hbm] * 4,
        out_specs=(vmem, vmem),
        scratch_shapes=[
            pltpu.VMEM((rows, positions, kv_width), BF16),
            pltpu.VMEM((rows, positions, kv_width), BF16),
            pltpu.VMEM((depth, units), F32),
            pltpu.VMEM((depth, units), F32),
            pltpu.VMEM((depth, units), BF16),
            pltpu.VMEM((depth, units), BF16),
            pltpu.VMEM((n_t, flat, HD), BF16),
            pltpu.VMEM((n_t, flat, HD), BF16),
            pltpu.VMEM((n_t, 8, HD), F32),
            pltpu.VMEM((n_t, 8, HD), F32),
            pltpu.VMEM((n_g, height, HD), BF16),
            pltpu.VMEM((n, height, HD), BF16),
            pltpu.VMEM((n * height, HD), F32),
            pltpu.VMEM((n_g, chunk, units), BF16),
            pltpu.VMEM((n_g, chunk, units), BF16),
            pltpu.VMEM((chunk, units), BF16),
            pltpu.VMEM((n_g, chunk, units), BF16),
            pltpu.VMEM((n_t, part_rows, depth), BF16),
            pltpu.VMEM((n_t, part_rows, depth), BF16),
            pltpu.VMEM((n_g * height, HD), F32),
            pltpu.VMEM((n_g, height, HD), BF16),
            dma((2, rows)),
            dma((2,)),
        ]
        + [dma((n_t,))] * 6
        + [dma((n,))] * 2
        + [dma((n_g,))] * 4
        + [dma((n_t,))] * 2
        + [dma((n,))] * 2,
        compiler_params=pltpu.CompilerParams(
            collective_id=0, has_side_effects=True, vmem_limit_bytes=32 * 1024 * 1024
        ),
    )(
        lengths,
        queries.reshape(rows, flat, HD),
        new_keys,
        new_values,
        residual.reshape(rows, flat, HD),
        norm_gain.reshape(heads, HD),
        cache_keys,
        cache_values,
        w_gate,
        w_down,
    )
    mlp = mlp.reshape(n_t, n_g, steps, heads // n_g, HD).transpose(0, 2, 1, 3, 4)
    total = summed.reshape(rows, steps, features).astype(F32) + mlp.reshape(
        rows, steps, features
    ).astype(F32)
    return total.astype(BF16)


def shards(n_g, n_t, *arrays):
    queries = arrays[0]
    rows, steps, features = queries.shape
    heads = features // HD
    even = (
        rows == n_t
        and heads % n_g == 0
        and n_g % 8 == 0
        and steps * (heads // n_g) == 8
        and steps * heads <= HD
        and (steps * n_t) % 8 == 0
    )
    if even:
        return moved_activations(n_g, n_t, *arrays)
    return gathered_weights(*arrays)


def solution(mesh):
    return jax.shard_map(
        functools.partial(shards, mesh.shape["grp"], mesh.shape["tp"]),
        mesh=mesh,
        in_specs=(
            P("grp", None, None),
            P("grp", "tp", None),
            P("grp", "tp", None),
            P("grp", None, None),
            P("grp", None, None),
            P("grp"),
            P("grp", None, None),
            P(),
            P("grp", "tp"),
            P("grp", "tp"),
        ),
        out_specs=P("grp", None, None),
        check_vma=False,
    )
```

```python
import functools

import jax
import jax.numpy as jnp
from jax import lax
from jax.experimental import pallas as pl
from jax.experimental.pallas import tpu as pltpu
from jax.sharding import PartitionSpec as P

HD = 128
KVH = 4


masked_score = -1e30


def merged_2(shard, axis, join):
    gathered = jax.tree.map(
        lambda a, kind: lax.all_gather(a.astype(kind), axis),
        shard,
        jax.tree.map(lambda a: jnp.bfloat16 if a.dtype == jnp.float32 else a.dtype, shard),
    )

    def take(source):
        return jax.tree.map(
            lambda a, own: lax.dynamic_index_in_dim(a, source, 0, False).astype(own.dtype),
            gathered,
            shard,
        )

    return lax.fori_loop(
        1, lax.axis_size(axis), lambda source, state: join(state, take(source)), take(0)
    )


def combine_parts(earlier, later):
    first_max, first_total, first_accum = earlier
    second_max, second_total, second_accum = later
    joint_max = jnp.maximum(first_max, second_max)
    first_factor = jnp.exp(first_max - joint_max)
    second_factor = jnp.exp(second_max - joint_max)
    joint_total = first_total * first_factor + second_total * second_factor
    joint_accum = first_accum * first_factor[..., None] + second_accum * second_factor[..., None]
    return (joint_max, joint_total, joint_accum)


def partial_softmax(scores, visible, value_heads, formula):
    scores = jnp.where(visible, scores, masked_score)
    highest = jnp.max(scores, axis=-1)
    weights = jnp.where(visible, jnp.exp(scores - highest[..., None]), 0.0)
    totals = jnp.sum(weights, axis=-1)
    accum = jnp.einsum(
        formula, weights.astype(jnp.bfloat16), value_heads, preferred_element_type=jnp.float32
    )
    return (highest, totals, accum)


def gathered_weights(
    queries,
    cache_keys,
    cache_values,
    new_keys,
    new_values,
    lengths,
    residual,
    norm_gain,
    w_gate,
    w_down,
):
    row_count, step_count, features = queries.shape
    positions = cache_keys.shape[1]
    per_group = features // (KVH * HD)
    inv_root = HD ** (-0.5)
    query_heads = queries.reshape(row_count, step_count, KVH, per_group, HD)
    key_heads = cache_keys.reshape(row_count, positions, KVH, HD)
    value_heads = cache_values.reshape(row_count, positions, KVH, HD)
    cached_scores = (
        jnp.einsum("rsjgd,rcjd->rsjgc", query_heads, key_heads, preferred_element_type=jnp.float32)
        * inv_root
    )
    offset = lax.axis_index("tp") * positions
    places = offset + lax.broadcasted_iota(jnp.int32, (row_count, positions), 1)
    visible = (places < lengths[:, None])[:, None, None, None, :]
    local_part = partial_softmax(cached_scores, visible, value_heads, "rsjgc,rcjd->rsjgd")
    merged = merged_2(local_part, "tp", combine_parts)
    fresh_key_heads = new_keys.reshape(row_count, step_count, KVH, HD)
    fresh_value_heads = new_values.reshape(row_count, step_count, KVH, HD)
    fresh_scores = (
        jnp.einsum(
            "rsjgd,rtjd->rsjgt", query_heads, fresh_key_heads, preferred_element_type=jnp.float32
        )
        * inv_root
    )
    causal = lax.broadcasted_iota(jnp.int32, (step_count, step_count), 0) >= lax.broadcasted_iota(
        jnp.int32, (step_count, step_count), 1
    )
    causal = causal[None, :, None, None, :]
    fresh_part = partial_softmax(fresh_scores, causal, fresh_value_heads, "rsjgt,rtjd->rsjgd")
    joint_max, joint_total, joint_accum = combine_parts(merged, fresh_part)
    context = (joint_accum / joint_total[..., None]).reshape(row_count, step_count, features)
    summed = residual.astype(jnp.float32) + context
    mean_square = jnp.mean(summed * summed, axis=-1, keepdims=True)
    normed = (summed * lax.rsqrt(mean_square + 1e-05) * norm_gain).astype(jnp.bfloat16)
    flat = normed.reshape(row_count * step_count, features)
    gate_policy, down_policy = (
        lax.all_gather(w_gate.astype(jnp.bfloat16), "grp", axis=0, tiled=True),
        lax.all_gather(w_down.astype(jnp.bfloat16), "grp", axis=0, tiled=True),
    )
    gate = jnp.dot(flat, gate_policy, preferred_element_type=jnp.float32)
    hidden = jax.nn.silu(gate).astype(jnp.bfloat16)
    partial_sum = lax.dot_general(
        hidden, down_policy, (((1,), (1,)), ((), ())), preferred_element_type=jnp.float32
    )
    mlp = lax.psum(partial_sum.astype(jnp.bfloat16), "tp").astype(jnp.float32)
    return (summed + mlp.reshape(row_count, step_count, features)).astype(jnp.bfloat16)


MESH = pl.DeviceIdType.MESH
BF16, F32 = jnp.bfloat16, jnp.float32


def layer_kernel(
    n_g,
    n_t,
    lengths_ref,
    q_hbm,
    nk_hbm,
    nv_hbm,
    res_hbm,
    gain_hbm,
    ck_hbm,
    cv_hbm,
    wg_hbm,
    wd_hbm,
    out_ref,
    q_in,
    nk_in,
    nv_in,
    res_in,
    gain,
    ck,
    cv,
    wg32,
    wd32,
    wg,
    wd,
    q_rows,
    res_rows,
    nk_rows,
    nv_rows,
    send_o,
    recv_o,
    send_l,
    recv_l,
    send_x,
    recv_x,
    x_rows,
    x_flat,
    send_g,
    recv_g,
    send_h,
    recv_h,
    send_m,
    recv_m,
    send_f,
    load_sem,
    o_send_sem,
    o_recv_sem,
    l_send_sem,
    l_recv_sem,
    m_send_sem,
    m_recv_sem,
    g_send_sem,
    g_recv_sem,
    h_send_sem,
    h_recv_sem,
    x_send_sem,
    x_recv_sem,
    f_send_sem,
    f_recv_sem,
):
    g, t = lax.axis_index("grp"), lax.axis_index("tp")
    rows, positions = ck.shape[0], ck.shape[1]
    steps = nk_in.shape[1]
    heads = gain.shape[0]
    units, depth = wg32.shape
    per_key = heads // KVH
    per_col = heads // n_g
    halves = per_key // per_col
    height = steps * per_col
    inv_root = HD ** (-0.5)
    group_rows = rows * steps
    half_t = n_t // 2

    loads = [
        pltpu.make_async_copy(source, target, load_sem.at[i])
        for i, (source, target) in enumerate(
            (
                (q_hbm, q_in),
                (ck_hbm, ck),
                (cv_hbm, cv),
                (nk_hbm, nk_in),
                (nv_hbm, nv_in),
                (res_hbm, res_in),
                (gain_hbm, gain),
                (wg_hbm, wg32),
                (wd_hbm, wd32),
            )
        )
    ]
    for load in loads:
        load.start()

    peer_g = [g] + [lax.rem(g + k, n_g) for k in range(1, n_g)]
    peer_t = [t] + [lax.rem(t + k, n_t) for k in range(1, n_t)]
    far_first = sorted(range(n_t), key=lambda k: (k == 0, abs(k - half_t)))

    barrier = pltpu.get_barrier_semaphore()
    for i in range(n_g):
        for k in range(n_t):
            if i or k:
                pl.semaphore_signal(
                    barrier, inc=1, device_id=(peer_g[i], peer_t[k]), device_id_type=MESH
                )

    def blocks_of(at):
        first = (at % 2) * n_t + at // 2
        return first, first + half_t

    mine = (lax.rem(t, 2) * n_t + t // 2, lax.rem(t, 2) * n_t + t // 2 + half_t)
    owner = lax.rem(lax.rem(g, n_t), half_t) * 2 + g // n_t

    def by_block(source, target):
        flat = jnp.concatenate([source[r].astype(F32) for r in range(rows)], axis=0)
        for h in range(heads):
            target[h // per_col, pl.ds(h % per_col, group_rows, stride=per_col), :] = flat[
                :, h * HD : (h + 1) * HD
            ]

    loads[0].wait()
    by_block(q_in, q_rows)
    loads[1].wait()
    lane_place = t * positions + lax.broadcasted_iota(jnp.int32, (halves * height, positions), 1)
    pieces, shown = [], []
    for r in range(rows):
        visible = (lane_place < lengths_ref[r]).astype(F32)
        for j in range(KVH):
            query = jnp.concatenate(
                [
                    q_rows[j * halves + i, r * height : (r + 1) * height]
                    for i in range(halves)
                ],
                axis=0,
            ).astype(BF16)
            pieces.append(
                lax.dot_general(
                    query,
                    ck[r, :, j * HD : (j + 1) * HD],
                    (((1,), (1,)), ((), ())),
                    preferred_element_type=F32,
                )
            )
            shown.append(visible)
    shown = jnp.concatenate(shown, axis=0) > 0.0
    scores = jnp.where(shown, jnp.concatenate(pieces, axis=0) * inv_root, masked_score)
    highest = jnp.max(scores, axis=-1, keepdims=True)
    weights = jnp.where(shown, jnp.exp(scores - highest), 0.0)
    total = jnp.sum(weights, axis=-1, keepdims=True)
    weights = weights.astype(BF16)
    loads[2].wait()
    tall = halves * height
    accum = jnp.concatenate(
        [
            jnp.dot(
                weights[(r * KVH + j) * tall : (r * KVH + j + 1) * tall],
                cv[r, :, j * HD : (j + 1) * HD],
                preferred_element_type=F32,
            )
            for r in range(rows)
            for j in range(KVH)
        ],
        axis=0,
    )
    some = total > 0.0
    safe = jnp.where(some, total, 1.0)
    means = accum / safe
    logs = jnp.where(some, highest + jnp.log(safe), masked_score)

    def of_owner(array, at):
        starts = [
            (r * KVH + b // halves) * tall + (b % halves) * height
            for b in blocks_of(at)
            for r in range(rows)
        ]
        return jnp.concatenate([array[i : i + height] for i in starts], axis=0)

    flat_rows = 2 * rows * height
    diagonal = lax.broadcasted_iota(jnp.int32, (flat_rows, HD), 0) == lax.broadcasted_iota(
        jnp.int32, (flat_rows, HD), 1
    )
    for at in range(n_t):
        send_o[at] = of_owner(means, at).astype(BF16)
        lanes = jnp.sum(jnp.where(diagonal, of_owner(logs, at), 0.0), axis=0, keepdims=True)
        send_l[at] = jnp.broadcast_to(lanes, send_l.shape[1:])

    def along_tp(k, source, target, send_sem, recv_sem):
        return pltpu.make_async_remote_copy(
            src_ref=source.at[peer_t[k]],
            dst_ref=target.at[t],
            send_sem=send_sem.at[k - 1],
            recv_sem=recv_sem.at[k - 1],
            device_id=(g, peer_t[k]),
            device_id_type=MESH,
        )

    pl.semaphore_wait(barrier, n_g * n_t - 1)
    row_copies = []
    for k in far_first[:-1]:
        row_copies.append(along_tp(k, send_o, recv_o, o_send_sem, o_recv_sem))
        row_copies.append(along_tp(k, send_l, recv_l, l_send_sem, l_recv_sem))
    for copy in row_copies:
        copy.start()
    recv_o[t] = send_o[t]
    recv_l[t] = send_l[t]

    for load in loads[3:]:
        load.wait()
    by_block(res_in, res_rows)
    for source, target in ((nk_in, nk_rows), (nv_in, nv_rows)):
        flat = jnp.concatenate([source[r].astype(F32) for r in range(rows)], axis=0)
        for j in range(KVH):
            target[j] = flat[:, j * HD : (j + 1) * HD]

    def new_tokens(tokens, at):
        out = []
        for b in mine:
            held = tokens[b // halves]
            for r in range(rows):
                place = r * steps + at
                out.append(jnp.broadcast_to(held[place : place + 1], (height, HD)))
        return jnp.concatenate(out, axis=0)

    query = jnp.concatenate([q_rows[b] for b in mine], axis=0)
    step_of = lax.broadcasted_iota(jnp.int32, (flat_rows, 1), 0) & (height - 1)
    seen = [step_of >= at * per_col for at in range(steps)]
    fresh = [
        jnp.where(
            seen[at],
            jnp.sum(query * new_tokens(nk_rows, at), axis=-1, keepdims=True) * inv_root,
            masked_score,
        )
        for at in range(steps)
    ]
    new_held = [new_tokens(nv_rows, at) for at in range(steps)]
    residual = jnp.concatenate([res_rows[b] for b in mine], axis=0)
    spare = jnp.zeros((wg.shape[0] - units, depth), F32)
    wg[...] = jnp.concatenate([wg32[...], spare], axis=0).astype(BF16)
    wd[...] = jnp.concatenate([wd32[...], spare], axis=0).astype(BF16)
    for copy in row_copies:
        copy.wait_recv()

    logs = [
        jnp.sum(jnp.where(diagonal, recv_l[i][0:1], 0.0), axis=-1, keepdims=True)
        for i in range(n_t)
    ]
    joint = functools.reduce(jnp.maximum, logs + fresh)
    total, accum = 0.0, 0.0
    for i in range(n_t):
        weight = jnp.exp(logs[i] - joint)
        total = total + weight
        accum = accum + weight * recv_o[i].astype(F32)
    for at in range(steps):
        weight = jnp.where(seen[at], jnp.exp(fresh[at] - joint), 0.0)
        total = total + weight
        accum = accum + weight.astype(BF16).astype(F32) * new_held[at]
    summed = (residual + accum / total).astype(BF16)
    block_rows = rows * height
    for i in range(2):
        send_x[i] = summed[i * block_rows : (i + 1) * block_rows]

    class Spread:
        def __init__(self, source, target, send_sem, recv_sem):
            self.refs = source, target, send_sem, recv_sem

        def each(self, action):
            source, target, send_sem, recv_sem = self.refs
            for k in far_first:
                for i in range(2):
                    copy = pltpu.make_async_remote_copy(
                        src_ref=source.at[i],
                        dst_ref=target.at[g],
                        send_sem=send_sem.at[i * n_t + k],
                        recv_sem=recv_sem.at[g],
                        device_id=(mine[i], peer_t[k]),
                        device_id_type=MESH,
                    )
                    if k:
                        action(copy)
                    else:
                        pl.when(mine[i] != g)(functools.partial(action, copy))

        def start(self):
            self.each(lambda copy: copy.start())
            source, target, _, _ = self.refs
            for i in range(2):

                @pl.when(mine[i] == g)
                def _():
                    target[g] = source[i]

        def wait_send(self):
            self.each(lambda copy: copy.wait_send())

        def wait_recv(self):
            source, target, send_sem, recv_sem = self.refs
            for i in range(n_g):
                copy = pltpu.make_async_remote_copy(
                    src_ref=source.at[0],
                    dst_ref=target.at[i],
                    send_sem=send_sem.at[0],
                    recv_sem=recv_sem.at[i],
                    device_id=(g, peer_t[1]),
                    device_id_type=MESH,
                )
                pl.when(jnp.logical_or(owner != t, g != i))(copy.wait_recv)

    x_spread = Spread(send_x, recv_x, x_send_sem, x_recv_sem)
    x_spread.start()
    x_spread.wait_recv()

    all_rows = n_g * group_rows
    x_rows[...] = recv_x[...].astype(F32).reshape(all_rows * per_col, HD)
    columns = [x_rows[pl.ds(c, all_rows, stride=per_col), :] for c in range(per_col)]
    squares = jnp.sum(
        functools.reduce(jnp.add, [c * c for c in columns]), axis=-1, keepdims=True
    )
    scaled = jnp.concatenate(
        [column * gain[pl.ds(g * per_col + c, 1)] for c, column in enumerate(columns)], axis=1
    ).astype(BF16)
    gate = lax.dot_general(
        scaled, wg[...], (((1,), (1,)), ((), ())), preferred_element_type=F32
    )
    spare_lane = lax.broadcasted_iota(jnp.int32, gate.shape, 1) >= units
    gate = jnp.where(spare_lane, squares, gate)
    for i in range(n_g):
        send_g[i] = gate[i * group_rows : (i + 1) * group_rows].astype(BF16)

    def along_grp(k, source, target, send_sem, recv_sem):
        return pltpu.make_async_remote_copy(
            src_ref=source,
            dst_ref=target.at[g],
            send_sem=send_sem.at[k - 1],
            recv_sem=recv_sem.at[k - 1],
            device_id=(peer_g[k], t),
            device_id_type=MESH,
        )

    gate_copies = [
        along_grp(k, send_g.at[peer_g[k]], recv_g, g_send_sem, g_recv_sem) for k in range(1, n_g)
    ]
    for copy in gate_copies:
        copy.start()
    recv_g[g] = send_g[g]
    x_flat[...] = jnp.concatenate(columns, axis=1).reshape(x_flat.shape)
    for copy in gate_copies:
        copy.wait_recv()
    whole = functools.reduce(jnp.add, [recv_g[i].astype(F32) for i in range(n_g)])
    square = whole[:, units : units + 1]
    whole = whole * lax.rsqrt(square / (heads * HD) + 1e-05)
    own_hidden = (whole / (1.0 + jnp.exp(-whole))).astype(BF16)

    send_h[...] = own_hidden
    hidden_copies = [
        along_grp(k, send_h, recv_h, h_send_sem, h_recv_sem) for k in range(1, n_g)
    ]
    for copy in hidden_copies:
        copy.start()
    recv_h[g] = own_hidden
    for copy in hidden_copies:
        copy.wait_recv()
    hidden = recv_h[...].astype(F32).reshape(all_rows, wd.shape[0]).astype(BF16)
    mlp = jnp.dot(hidden, wd[...], preferred_element_type=F32)

    for at in range(n_t):
        send_m[at] = jnp.concatenate(
            [mlp[b * group_rows : (b + 1) * group_rows] for b in blocks_of(at)], axis=0
        ).astype(BF16)
    mlp_copies = [along_tp(k, send_m, recv_m, m_send_sem, m_recv_sem) for k in far_first[:-1]]
    for copy in mlp_copies:
        copy.start()
    recv_m[t] = send_m[t]
    for copy in mlp_copies:
        copy.wait_recv()
    done = functools.reduce(jnp.add, [recv_m[i].astype(F32) for i in range(n_t)])
    for i in range(2):
        send_f[i] = (x_flat[mine[i]] + done[i * group_rows : (i + 1) * group_rows]).astype(BF16)

    f_spread = Spread(send_f, out_ref, f_send_sem, f_recv_sem)
    f_spread.start()
    for copy in row_copies + gate_copies + hidden_copies + mlp_copies:
        copy.wait_send()
    x_spread.wait_send()
    f_spread.wait_recv()
    f_spread.wait_send()


def moved_activations(
    n_g,
    n_t,
    queries,
    cache_keys,
    cache_values,
    new_keys,
    new_values,
    lengths,
    residual,
    norm_gain,
    w_gate,
    w_down,
):
    rows, steps, features = queries.shape
    positions, kv_width = cache_keys.shape[1:]
    depth, units = w_gate.shape
    heads = features // HD
    per_col = heads // n_g
    height = steps * per_col
    group_rows = rows * steps
    wide = (units // HD + 1) * HD
    hbm = pl.BlockSpec(memory_space=pltpu.HBM)
    dma = pltpu.SemaphoreType.DMA
    out = pl.pallas_call(
        functools.partial(layer_kernel, n_g, n_t),
        out_shape=jax.ShapeDtypeStruct((n_g, group_rows, depth), BF16),
        in_specs=[pl.BlockSpec(memory_space=pltpu.SMEM)] + [hbm] * 9,
        out_specs=pl.BlockSpec(memory_space=pltpu.VMEM),
        scratch_shapes=[
            pltpu.VMEM(queries.shape, BF16),
            pltpu.VMEM(new_keys.shape, BF16),
            pltpu.VMEM(new_values.shape, BF16),
            pltpu.VMEM(residual.shape, BF16),
            pltpu.VMEM((heads, HD), F32),
            pltpu.VMEM(cache_keys.shape, BF16),
            pltpu.VMEM(cache_values.shape, BF16),
            pltpu.VMEM((units, depth), F32),
            pltpu.VMEM((units, depth), F32),
            pltpu.VMEM((wide, depth), BF16),
            pltpu.VMEM((wide, depth), BF16),
            pltpu.VMEM((n_g, rows * height, HD), F32),
            pltpu.VMEM((n_g, rows * height, HD), F32),
            pltpu.VMEM((KVH, group_rows, HD), F32),
            pltpu.VMEM((KVH, group_rows, HD), F32),
            pltpu.VMEM((n_t, 2 * rows * height, HD), BF16),
            pltpu.VMEM((n_t, 2 * rows * height, HD), BF16),
            pltpu.VMEM((n_t, 8, HD), F32),
            pltpu.VMEM((n_t, 8, HD), F32),
            pltpu.VMEM((2, rows * height, HD), BF16),
            pltpu.VMEM((n_g, rows * height, HD), BF16),
            pltpu.VMEM((n_g * rows * height, HD), F32),
            pltpu.VMEM((n_g, group_rows, depth), F32),
            pltpu.VMEM((n_g, group_rows, wide), BF16),
            pltpu.VMEM((n_g, group_rows, wide), BF16),
            pltpu.VMEM((group_rows, wide), BF16),
            pltpu.VMEM((n_g, group_rows, wide), BF16),
            pltpu.VMEM((n_t, 2 * group_rows, depth), BF16),
            pltpu.VMEM((n_t, 2 * group_rows, depth), BF16),
            pltpu.VMEM((2, group_rows, depth), BF16),
            dma((9,)),
        ]
        + [dma((n_t,))] * 6
        + [dma((n_g,))] * 8,
        compiler_params=pltpu.CompilerParams(
            collective_id=0, has_side_effects=True, vmem_limit_bytes=56 * 1024 * 1024
        ),
    )(
        lengths,
        queries,
        new_keys,
        new_values,
        residual,
        norm_gain.reshape(heads, HD),
        cache_keys,
        cache_values,
        w_gate.T,
        w_down.T,
    )
    return out.transpose(1, 0, 2).reshape(rows, steps, features)


def shards(n_g, n_t, *arrays):
    queries, cache_keys = arrays[0], arrays[1]
    rows, steps, features = queries.shape
    heads = features // HD
    kv_heads = cache_keys.shape[2] // HD
    even = (
        n_g == 2 * n_t
        and n_t % 2 == 0
        and heads % n_g == 0
        and n_g % kv_heads == 0
        and steps * (heads // n_g) == 8
        and rows * steps == 8
    )
    if even:
        return moved_activations(n_g, n_t, *arrays)
    return gathered_weights(*arrays)


def solution(mesh):
    return jax.shard_map(
        functools.partial(shards, mesh.shape["grp"], mesh.shape["tp"]),
        mesh=mesh,
        in_specs=(
            P("grp", None, None),
            P("grp", "tp", None),
            P("grp", "tp", None),
            P("grp", None, None),
            P("grp", None, None),
            P("grp"),
            P("grp", None, None),
            P(),
            P("grp", "tp"),
            P("grp", "tp"),
        ),
        out_specs=P("grp", None, None),
        check_vma=False,
    )
```

```python
import functools

import jax
import jax.numpy as jnp
from jax import lax
from jax.experimental import pallas as pl
from jax.experimental.pallas import tpu as pltpu
from jax.sharding import PartitionSpec as P

HD = 128
KVH = 4


masked_score = -1e30


def merged_2(shard, axis, join):
    gathered = jax.tree.map(
        lambda a, kind: lax.all_gather(a.astype(kind), axis),
        shard,
        jax.tree.map(lambda a: jnp.bfloat16 if a.dtype == jnp.float32 else a.dtype, shard),
    )

    def take(source):
        return jax.tree.map(
            lambda a, own: lax.dynamic_index_in_dim(a, source, 0, False).astype(own.dtype),
            gathered,
            shard,
        )

    return lax.fori_loop(
        1, lax.axis_size(axis), lambda source, state: join(state, take(source)), take(0)
    )


def combine_parts(earlier, later):
    first_max, first_total, first_accum = earlier
    second_max, second_total, second_accum = later
    joint_max = jnp.maximum(first_max, second_max)
    first_factor = jnp.exp(first_max - joint_max)
    second_factor = jnp.exp(second_max - joint_max)
    joint_total = first_total * first_factor + second_total * second_factor
    joint_accum = first_accum * first_factor[..., None] + second_accum * second_factor[..., None]
    return (joint_max, joint_total, joint_accum)


def partial_softmax(scores, visible, value_heads, formula):
    scores = jnp.where(visible, scores, masked_score)
    highest = jnp.max(scores, axis=-1)
    weights = jnp.where(visible, jnp.exp(scores - highest[..., None]), 0.0)
    totals = jnp.sum(weights, axis=-1)
    accum = jnp.einsum(
        formula, weights.astype(jnp.bfloat16), value_heads, preferred_element_type=jnp.float32
    )
    return (highest, totals, accum)


def gathered_weights(
    queries,
    cache_keys,
    cache_values,
    new_keys,
    new_values,
    lengths,
    residual,
    norm_gain,
    w_gate,
    w_down,
):
    row_count, step_count, features = queries.shape
    positions = cache_keys.shape[1]
    per_group = features // (KVH * HD)
    inv_root = HD ** (-0.5)
    query_heads = queries.reshape(row_count, step_count, KVH, per_group, HD)
    key_heads = cache_keys.reshape(row_count, positions, KVH, HD)
    value_heads = cache_values.reshape(row_count, positions, KVH, HD)
    cached_scores = (
        jnp.einsum("rsjgd,rcjd->rsjgc", query_heads, key_heads, preferred_element_type=jnp.float32)
        * inv_root
    )
    offset = lax.axis_index("tp") * positions
    places = offset + lax.broadcasted_iota(jnp.int32, (row_count, positions), 1)
    visible = (places < lengths[:, None])[:, None, None, None, :]
    local_part = partial_softmax(cached_scores, visible, value_heads, "rsjgc,rcjd->rsjgd")
    merged = merged_2(local_part, "tp", combine_parts)
    fresh_key_heads = new_keys.reshape(row_count, step_count, KVH, HD)
    fresh_value_heads = new_values.reshape(row_count, step_count, KVH, HD)
    fresh_scores = (
        jnp.einsum(
            "rsjgd,rtjd->rsjgt", query_heads, fresh_key_heads, preferred_element_type=jnp.float32
        )
        * inv_root
    )
    causal = lax.broadcasted_iota(jnp.int32, (step_count, step_count), 0) >= lax.broadcasted_iota(
        jnp.int32, (step_count, step_count), 1
    )
    causal = causal[None, :, None, None, :]
    fresh_part = partial_softmax(fresh_scores, causal, fresh_value_heads, "rsjgt,rtjd->rsjgd")
    joint_max, joint_total, joint_accum = combine_parts(merged, fresh_part)
    context = (joint_accum / joint_total[..., None]).reshape(row_count, step_count, features)
    summed = residual.astype(jnp.float32) + context
    mean_square = jnp.mean(summed * summed, axis=-1, keepdims=True)
    normed = (summed * lax.rsqrt(mean_square + 1e-05) * norm_gain).astype(jnp.bfloat16)
    flat = normed.reshape(row_count * step_count, features)
    gate_policy, down_policy = (
        lax.all_gather(w_gate.astype(jnp.bfloat16), "grp", axis=0, tiled=True),
        lax.all_gather(w_down.astype(jnp.bfloat16), "grp", axis=0, tiled=True),
    )
    gate = jnp.dot(flat, gate_policy, preferred_element_type=jnp.float32)
    hidden = jax.nn.silu(gate).astype(jnp.bfloat16)
    partial_sum = lax.dot_general(
        hidden, down_policy, (((1,), (1,)), ((), ())), preferred_element_type=jnp.float32
    )
    mlp = lax.psum(partial_sum.astype(jnp.bfloat16), "tp").astype(jnp.float32)
    return (summed + mlp.reshape(row_count, step_count, features)).astype(jnp.bfloat16)


MESH = pl.DeviceIdType.MESH
BF16, F32 = jnp.bfloat16, jnp.float32


def layer_kernel(
    n_g,
    n_t,
    lengths_ref,
    q_hbm,
    nk_hbm,
    nv_hbm,
    res_hbm,
    gain_hbm,
    ck_hbm,
    cv_hbm,
    wg_hbm,
    wd_hbm,
    out_ref,
    q_in,
    nk_in,
    nv_in,
    res_in,
    gain,
    ck,
    cv,
    wg32,
    wd32,
    wg,
    wd,
    q_rows,
    res_rows,
    nk_rows,
    nv_rows,
    send_o,
    recv_o,
    send_x,
    recv_x,
    x_rows,
    x_flat,
    send_g,
    recv_g,
    send_h,
    recv_h,
    send_m,
    recv_m,
    send_f,
    load_sem,
    o_send_sem,
    o_recv_sem,
    m_send_sem,
    m_recv_sem,
    g_send_sem,
    g_recv_sem,
    h_send_sem,
    h_recv_sem,
    x_send_sem,
    x_recv_sem,
    f_send_sem,
    f_recv_sem,
):
    g, t = lax.axis_index("grp"), lax.axis_index("tp")
    rows, positions = ck.shape[0], ck.shape[1]
    steps = nk_in.shape[1]
    heads = gain.shape[0]
    units, depth = wg32.shape
    per_key = heads // KVH
    per_col = heads // n_g
    halves = per_key // per_col
    height = steps * per_col
    inv_root = HD ** (-0.5)
    group_rows = rows * steps
    half_t = n_t // 2

    loads = [
        pltpu.make_async_copy(source, target, load_sem.at[i])
        for i, (source, target) in enumerate(
            (
                (q_hbm, q_in),
                (ck_hbm, ck),
                (cv_hbm, cv),
                (nk_hbm, nk_in),
                (nv_hbm, nv_in),
                (res_hbm, res_in),
                (gain_hbm, gain),
                (wg_hbm, wg32),
                (wd_hbm, wd32),
            )
        )
    ]
    for load in loads:
        load.start()

    peer_g = [g] + [lax.rem(g + k, n_g) for k in range(1, n_g)]
    peer_t = [t] + [lax.rem(t + k, n_t) for k in range(1, n_t)]
    far_first = sorted(range(n_t), key=lambda k: (k == 0, abs(k - half_t)))

    barrier = pltpu.get_barrier_semaphore()
    for i in range(n_g):
        for k in range(n_t):
            if i or k:
                pl.semaphore_signal(
                    barrier, inc=1, device_id=(peer_g[i], peer_t[k]), device_id_type=MESH
                )

    def blocks_of(at):
        first = (at % 2) * n_t + at // 2
        return first, first + half_t

    mine = (lax.rem(t, 2) * n_t + t // 2, lax.rem(t, 2) * n_t + t // 2 + half_t)

    def by_block(source, target):
        flat = jnp.concatenate([source[r].astype(F32) for r in range(rows)], axis=0)
        for h in range(heads):
            target[h // per_col, pl.ds(h % per_col, group_rows, stride=per_col), :] = flat[
                :, h * HD : (h + 1) * HD
            ]

    loads[0].wait()
    by_block(q_in, q_rows)
    loads[1].wait()
    lane_place = t * positions + lax.broadcasted_iota(jnp.int32, (halves * height, positions), 1)
    pieces, shown = [], []
    tall = halves * height
    blank = jnp.zeros((tall, HD), F32)
    for r in range(rows):
        visible = (lane_place < lengths_ref[r]).astype(F32)
        query = []
        for j in range(KVH):
            own = jnp.concatenate(
                [
                    q_rows[j * halves + i, r * height : (r + 1) * height]
                    for i in range(halves)
                ],
                axis=0,
            )
            query.append(jnp.concatenate([blank] * j + [own] + [blank] * (KVH - 1 - j), axis=1))
            shown.append(visible)
        pieces.append(
            lax.dot_general(
                jnp.concatenate(query, axis=0).astype(BF16),
                ck[r],
                (((1,), (1,)), ((), ())),
                preferred_element_type=F32,
            )
        )
    shown = jnp.concatenate(shown, axis=0) > 0.0
    scores = jnp.where(shown, jnp.concatenate(pieces, axis=0) * inv_root, masked_score)
    highest = jnp.max(scores, axis=-1, keepdims=True)
    weights = jnp.where(shown, jnp.exp(scores - highest), 0.0)
    total = jnp.sum(weights, axis=-1, keepdims=True)
    weights = weights.astype(BF16)
    loads[2].wait()
    accum = []
    for r in range(rows):
        wide = jnp.dot(
            weights[r * KVH * tall : (r + 1) * KVH * tall], cv[r], preferred_element_type=F32
        )
        for j in range(KVH):
            accum.append(wide[j * tall : (j + 1) * tall, j * HD : (j + 1) * HD])
    some = total > 0.0
    safe = jnp.where(some, total, 1.0)
    means = jnp.concatenate(accum, axis=0) / safe
    logs = jnp.where(some, highest + jnp.log(safe), masked_score)

    def of_owner(array, at):
        starts = [
            (r * KVH + b // halves) * tall + (b % halves) * height
            for b in blocks_of(at)
            for r in range(rows)
        ]
        return jnp.concatenate([array[i : i + height] for i in starts], axis=0)

    flat_rows = 2 * rows * height
    diagonal = lax.broadcasted_iota(jnp.int32, (flat_rows, HD), 0) == lax.broadcasted_iota(
        jnp.int32, (flat_rows, HD), 1
    )
    place = lax.broadcasted_iota(jnp.int32, (send_o.shape[1] - flat_rows, HD), 0)
    for at in range(n_t):
        lanes = jnp.sum(jnp.where(diagonal, of_owner(logs, at), 0.0), axis=0, keepdims=True)
        high = lanes.astype(BF16).astype(F32)
        middle = (lanes - high).astype(BF16).astype(F32)
        low = lanes - high - middle
        terms = jnp.where(place == 0, high, jnp.where(place == 1, middle, low))
        send_o[at] = jnp.concatenate([of_owner(means, at), terms], axis=0).astype(BF16)

    def along_tp(k, source, target, send_sem, recv_sem):
        return pltpu.make_async_remote_copy(
            src_ref=source.at[peer_t[k]],
            dst_ref=target.at[t],
            send_sem=send_sem.at[k - 1],
            recv_sem=recv_sem.at[k - 1],
            device_id=(g, peer_t[k]),
            device_id_type=MESH,
        )

    pl.semaphore_wait(barrier, n_g * n_t - 1)
    row_copies = []
    for k in far_first[:-1]:
        row_copies.append(along_tp(k, send_o, recv_o, o_send_sem, o_recv_sem))
    for copy in row_copies:
        copy.start()
    recv_o[t] = send_o[t]

    for load in loads[3:]:
        load.wait()
    by_block(res_in, res_rows)
    for source, target in ((nk_in, nk_rows), (nv_in, nv_rows)):
        flat = jnp.concatenate([source[r].astype(F32) for r in range(rows)], axis=0)
        for j in range(KVH):
            target[j] = flat[:, j * HD : (j + 1) * HD]

    def new_tokens(tokens, at):
        out = []
        for b in mine:
            held = tokens[b // halves]
            for r in range(rows):
                place = r * steps + at
                out.append(jnp.broadcast_to(held[place : place + 1], (height, HD)))
        return jnp.concatenate(out, axis=0)

    query = jnp.concatenate([q_rows[b] for b in mine], axis=0)
    step_of = lax.broadcasted_iota(jnp.int32, (flat_rows, 1), 0) & (height - 1)
    seen = [step_of >= at * per_col for at in range(steps)]
    fresh = [
        jnp.where(
            seen[at],
            jnp.sum(query * new_tokens(nk_rows, at), axis=-1, keepdims=True) * inv_root,
            masked_score,
        )
        for at in range(steps)
    ]
    new_held = [new_tokens(nv_rows, at) for at in range(steps)]
    residual = jnp.concatenate([res_rows[b] for b in mine], axis=0)
    spare = jnp.zeros((wg.shape[0] - units, depth), F32)
    wg[...] = jnp.concatenate([wg32[...], spare], axis=0).astype(BF16)
    wd[...] = jnp.concatenate([wd32[...], spare], axis=0).astype(BF16)
    for copy in row_copies:
        copy.wait_recv()

    logs = [
        jnp.sum(jnp.where(diagonal, terms[0:1] + terms[1:2] + terms[2:3], 0.0), axis=-1, keepdims=True)
        for terms in [recv_o[i, flat_rows:].astype(F32) for i in range(n_t)]
    ]
    joint = functools.reduce(jnp.maximum, logs + fresh)
    total, accum = 0.0, 0.0
    for i in range(n_t):
        weight = jnp.exp(logs[i] - joint)
        total = total + weight
        accum = accum + weight * recv_o[i, :flat_rows].astype(F32)
    for at in range(steps):
        weight = jnp.where(seen[at], jnp.exp(fresh[at] - joint), 0.0)
        total = total + weight
        accum = accum + weight.astype(BF16).astype(F32) * new_held[at]
    summed = (residual + accum / total).astype(BF16)
    block_rows = rows * height
    for i in range(2):
        send_x[i] = summed[i * block_rows : (i + 1) * block_rows]

    class Spread:
        def __init__(self, source, target, send_sem, recv_sem):
            self.refs = source, target, send_sem, recv_sem

        def each(self, action):
            source, target, send_sem, recv_sem = self.refs
            for k in far_first:
                for i in range(2):
                    copy = pltpu.make_async_remote_copy(
                        src_ref=source.at[i],
                        dst_ref=target(g),
                        send_sem=send_sem.at[i * n_t + k],
                        recv_sem=recv_sem.at[g],
                        device_id=(mine[i], peer_t[k]),
                        device_id_type=MESH,
                    )
                    if k:
                        action(copy)
                    else:
                        pl.when(mine[i] != g)(functools.partial(action, copy))

        def start(self):
            self.each(lambda copy: copy.start())
            source, target, _, recv_sem = self.refs
            for i in range(2):
                here = pltpu.make_async_copy(source.at[i], target(g), recv_sem.at[g])
                pl.when(mine[i] == g)(here.start)

        def wait_send(self):
            self.each(lambda copy: copy.wait_send())

        def wait_recv(self):
            source, target, _, recv_sem = self.refs
            for i in range(n_g):
                pltpu.make_async_copy(source.at[0], target(i), recv_sem.at[i]).wait()

    x_spread = Spread(send_x, lambda i: recv_x.at[i], x_send_sem, x_recv_sem)
    x_spread.start()
    x_spread.wait_recv()

    all_rows = n_g * group_rows
    x_rows[...] = recv_x[...].astype(F32).reshape(all_rows * per_col, HD)
    columns = [x_rows[pl.ds(c, all_rows, stride=per_col), :] for c in range(per_col)]
    squares = jnp.sum(
        functools.reduce(jnp.add, [c * c for c in columns]), axis=-1, keepdims=True
    )
    scaled = jnp.concatenate(
        [column * gain[pl.ds(g * per_col + c, 1)] for c, column in enumerate(columns)], axis=1
    ).astype(BF16)
    gate = lax.dot_general(
        scaled, wg[...], (((1,), (1,)), ((), ())), preferred_element_type=F32
    )
    spare_lane = lax.broadcasted_iota(jnp.int32, gate.shape, 1) >= units
    gate = jnp.where(spare_lane, squares, gate)
    for i in range(n_g):
        send_g[i] = gate[i * group_rows : (i + 1) * group_rows].astype(BF16)

    def along_grp(k, source, target, send_sem, recv_sem):
        return pltpu.make_async_remote_copy(
            src_ref=source,
            dst_ref=target.at[g],
            send_sem=send_sem.at[k - 1],
            recv_sem=recv_sem.at[k - 1],
            device_id=(peer_g[k], t),
            device_id_type=MESH,
        )

    gate_copies = [
        along_grp(k, send_g.at[peer_g[k]], recv_g, g_send_sem, g_recv_sem) for k in range(1, n_g)
    ]
    for copy in gate_copies:
        copy.start()
    recv_g[g] = send_g[g]
    x_flat[...] = jnp.concatenate(columns, axis=1).reshape(x_flat.shape)
    for copy in gate_copies:
        copy.wait_recv()
    whole = functools.reduce(jnp.add, [recv_g[i].astype(F32) for i in range(n_g)])
    square = whole[:, units : units + 1]
    whole = whole * lax.rsqrt(square / (heads * HD) + 1e-05)
    own_hidden = (whole / (1.0 + jnp.exp(-whole))).astype(BF16)

    send_h[...] = own_hidden
    hidden_copies = [
        along_grp(k, send_h, recv_h, h_send_sem, h_recv_sem) for k in range(1, n_g)
    ]
    for copy in hidden_copies:
        copy.start()
    recv_h[g] = own_hidden
    for copy in hidden_copies:
        copy.wait_recv()
    hidden = recv_h[...].astype(F32).reshape(all_rows, wd.shape[0]).astype(BF16)
    mlp = jnp.dot(hidden, wd[...], preferred_element_type=F32)

    for at in range(n_t):
        send_m[at] = jnp.concatenate(
            [mlp[b * group_rows : (b + 1) * group_rows] for b in blocks_of(at)], axis=0
        ).astype(BF16)
    mlp_copies = [along_tp(k, send_m, recv_m, m_send_sem, m_recv_sem) for k in far_first[:-1]]
    for copy in mlp_copies:
        copy.start()
    recv_m[t] = send_m[t]
    for copy in mlp_copies:
        copy.wait_recv()
    done = functools.reduce(jnp.add, [recv_m[i].astype(F32) for i in range(n_t)])
    for i in range(2):
        send_f[i] = (x_flat[mine[i]] + done[i * group_rows : (i + 1) * group_rows]).astype(BF16)

    def out_columns(i):
        return out_ref.at[:, pl.ds(pl.multiple_of(i * depth, depth), depth)]

    f_spread = Spread(send_f, out_columns, f_send_sem, f_recv_sem)
    f_spread.start()
    for copy in row_copies + gate_copies + hidden_copies + mlp_copies:
        copy.wait_send()
    x_spread.wait_send()
    f_spread.wait_recv()
    f_spread.wait_send()


def moved_activations(
    n_g,
    n_t,
    queries,
    cache_keys,
    cache_values,
    new_keys,
    new_values,
    lengths,
    residual,
    norm_gain,
    w_gate,
    w_down,
):
    rows, steps, features = queries.shape
    positions, kv_width = cache_keys.shape[1:]
    depth, units = w_gate.shape
    heads = features // HD
    per_col = heads // n_g
    height = steps * per_col
    group_rows = rows * steps
    wide = (units // HD + 1) * HD
    hbm = pl.BlockSpec(memory_space=pltpu.HBM)
    dma = pltpu.SemaphoreType.DMA
    out = pl.pallas_call(
        functools.partial(layer_kernel, n_g, n_t),
        out_shape=jax.ShapeDtypeStruct((group_rows, features), BF16),
        in_specs=[pl.BlockSpec(memory_space=pltpu.SMEM)] + [hbm] * 9,
        out_specs=hbm,
        scratch_shapes=[
            pltpu.VMEM(queries.shape, BF16),
            pltpu.VMEM(new_keys.shape, BF16),
            pltpu.VMEM(new_values.shape, BF16),
            pltpu.VMEM(residual.shape, BF16),
            pltpu.VMEM((heads, HD), F32),
            pltpu.VMEM(cache_keys.shape, BF16),
            pltpu.VMEM(cache_values.shape, BF16),
            pltpu.VMEM((units, depth), F32),
            pltpu.VMEM((units, depth), F32),
            pltpu.VMEM((wide, depth), BF16),
            pltpu.VMEM((wide, depth), BF16),
            pltpu.VMEM((n_g, rows * height, HD), F32),
            pltpu.VMEM((n_g, rows * height, HD), F32),
            pltpu.VMEM((KVH, group_rows, HD), F32),
            pltpu.VMEM((KVH, group_rows, HD), F32),
            pltpu.VMEM((n_t, 2 * rows * height + 16, HD), BF16),
            pltpu.VMEM((n_t, 2 * rows * height + 16, HD), BF16),
            pltpu.VMEM((2, rows * height, HD), BF16),
            pltpu.VMEM((n_g, rows * height, HD), BF16),
            pltpu.VMEM((n_g * rows * height, HD), F32),
            pltpu.VMEM((n_g, group_rows, depth), F32),
            pltpu.VMEM((n_g, group_rows, wide), BF16),
            pltpu.VMEM((n_g, group_rows, wide), BF16),
            pltpu.VMEM((group_rows, wide), BF16),
            pltpu.VMEM((n_g, group_rows, wide), BF16),
            pltpu.VMEM((n_t, 2 * group_rows, depth), BF16),
            pltpu.VMEM((n_t, 2 * group_rows, depth), BF16),
            pltpu.VMEM((2, group_rows, depth), BF16),
            dma((9,)),
        ]
        + [dma((n_t,))] * 4
        + [dma((n_g,))] * 8,
        compiler_params=pltpu.CompilerParams(
            collective_id=0, has_side_effects=True, vmem_limit_bytes=56 * 1024 * 1024
        ),
    )(
        lengths,
        queries,
        new_keys,
        new_values,
        residual,
        norm_gain.reshape(heads, HD),
        cache_keys,
        cache_values,
        w_gate.T,
        w_down.T,
    )
    return out.reshape(rows, steps, features)


def shards(n_g, n_t, *arrays):
    queries, cache_keys = arrays[0], arrays[1]
    rows, steps, features = queries.shape
    heads = features // HD
    kv_heads = cache_keys.shape[2] // HD
    even = (
        n_g == 2 * n_t
        and n_t % 2 == 0
        and heads % n_g == 0
        and n_g % kv_heads == 0
        and steps * (heads // n_g) == 8
        and rows * steps == 8
    )
    if even:
        return moved_activations(n_g, n_t, *arrays)
    return gathered_weights(*arrays)


def solution(mesh):
    return jax.shard_map(
        functools.partial(shards, mesh.shape["grp"], mesh.shape["tp"]),
        mesh=mesh,
        in_specs=(
            P("grp", None, None),
            P("grp", "tp", None),
            P("grp", "tp", None),
            P("grp", None, None),
            P("grp", None, None),
            P("grp"),
            P("grp", None, None),
            P(),
            P("grp", "tp"),
            P("grp", "tp"),
        ),
        out_specs=P("grp", None, None),
        check_vma=False,
    )
```

```python
import functools

import jax
import jax.numpy as jnp
from jax import lax
from jax.experimental import pallas as pl
from jax.experimental.pallas import tpu as pltpu
from jax.sharding import PartitionSpec as P

HD = 128
KVH = 4


masked_score = -1e30


def merged_2(shard, axis, join):
    gathered = jax.tree.map(
        lambda a, kind: lax.all_gather(a.astype(kind), axis),
        shard,
        jax.tree.map(lambda a: jnp.bfloat16 if a.dtype == jnp.float32 else a.dtype, shard),
    )

    def take(source):
        return jax.tree.map(
            lambda a, own: lax.dynamic_index_in_dim(a, source, 0, False).astype(own.dtype),
            gathered,
            shard,
        )

    return lax.fori_loop(
        1, lax.axis_size(axis), lambda source, state: join(state, take(source)), take(0)
    )


def combine_parts(earlier, later):
    first_max, first_total, first_accum = earlier
    second_max, second_total, second_accum = later
    joint_max = jnp.maximum(first_max, second_max)
    first_factor = jnp.exp(first_max - joint_max)
    second_factor = jnp.exp(second_max - joint_max)
    joint_total = first_total * first_factor + second_total * second_factor
    joint_accum = first_accum * first_factor[..., None] + second_accum * second_factor[..., None]
    return (joint_max, joint_total, joint_accum)


def partial_softmax(scores, visible, value_heads, formula):
    scores = jnp.where(visible, scores, masked_score)
    highest = jnp.max(scores, axis=-1)
    weights = jnp.where(visible, jnp.exp(scores - highest[..., None]), 0.0)
    totals = jnp.sum(weights, axis=-1)
    accum = jnp.einsum(
        formula, weights.astype(jnp.bfloat16), value_heads, preferred_element_type=jnp.float32
    )
    return (highest, totals, accum)


def gathered_weights(
    queries,
    cache_keys,
    cache_values,
    new_keys,
    new_values,
    lengths,
    residual,
    norm_gain,
    w_gate,
    w_down,
):
    row_count, step_count, features = queries.shape
    positions = cache_keys.shape[1]
    per_group = features // (KVH * HD)
    inv_root = HD ** (-0.5)
    query_heads = queries.reshape(row_count, step_count, KVH, per_group, HD)
    key_heads = cache_keys.reshape(row_count, positions, KVH, HD)
    value_heads = cache_values.reshape(row_count, positions, KVH, HD)
    cached_scores = (
        jnp.einsum("rsjgd,rcjd->rsjgc", query_heads, key_heads, preferred_element_type=jnp.float32)
        * inv_root
    )
    offset = lax.axis_index("tp") * positions
    places = offset + lax.broadcasted_iota(jnp.int32, (row_count, positions), 1)
    visible = (places < lengths[:, None])[:, None, None, None, :]
    local_part = partial_softmax(cached_scores, visible, value_heads, "rsjgc,rcjd->rsjgd")
    merged = merged_2(local_part, "tp", combine_parts)
    fresh_key_heads = new_keys.reshape(row_count, step_count, KVH, HD)
    fresh_value_heads = new_values.reshape(row_count, step_count, KVH, HD)
    fresh_scores = (
        jnp.einsum(
            "rsjgd,rtjd->rsjgt", query_heads, fresh_key_heads, preferred_element_type=jnp.float32
        )
        * inv_root
    )
    causal = lax.broadcasted_iota(jnp.int32, (step_count, step_count), 0) >= lax.broadcasted_iota(
        jnp.int32, (step_count, step_count), 1
    )
    causal = causal[None, :, None, None, :]
    fresh_part = partial_softmax(fresh_scores, causal, fresh_value_heads, "rsjgt,rtjd->rsjgd")
    joint_max, joint_total, joint_accum = combine_parts(merged, fresh_part)
    context = (joint_accum / joint_total[..., None]).reshape(row_count, step_count, features)
    summed = residual.astype(jnp.float32) + context
    mean_square = jnp.mean(summed * summed, axis=-1, keepdims=True)
    normed = (summed * lax.rsqrt(mean_square + 1e-05) * norm_gain).astype(jnp.bfloat16)
    flat = normed.reshape(row_count * step_count, features)
    gate_policy, down_policy = (
        lax.all_gather(w_gate.astype(jnp.bfloat16), "grp", axis=0, tiled=True),
        lax.all_gather(w_down.astype(jnp.bfloat16), "grp", axis=0, tiled=True),
    )
    gate = jnp.dot(flat, gate_policy, preferred_element_type=jnp.float32)
    hidden = jax.nn.silu(gate).astype(jnp.bfloat16)
    partial_sum = lax.dot_general(
        hidden, down_policy, (((1,), (1,)), ((), ())), preferred_element_type=jnp.float32
    )
    mlp = lax.psum(partial_sum.astype(jnp.bfloat16), "tp").astype(jnp.float32)
    return (summed + mlp.reshape(row_count, step_count, features)).astype(jnp.bfloat16)


MESH = pl.DeviceIdType.MESH
BF16, F32 = jnp.bfloat16, jnp.float32


def layer_kernel(
    n_g,
    n_t,
    lengths_ref,
    q_hbm,
    nk_hbm,
    nv_hbm,
    res_hbm,
    gain_hbm,
    ck_hbm,
    cv_hbm,
    wg_hbm,
    wd_hbm,
    out_ref,
    q_in,
    nk_in,
    nv_in,
    res_in,
    gain,
    ck,
    cv,
    wg32,
    wd32,
    wg,
    wd,
    q_rows,
    res_rows,
    nk_rows,
    nv_rows,
    send_o,
    recv_o,
    send_x,
    recv_x,
    x_rows,
    x_flat,
    send_g,
    recv_g,
    send_h,
    recv_h,
    send_m,
    recv_m,
    send_f,
    load_sem,
    o_send_sem,
    o_recv_sem,
    m_send_sem,
    m_recv_sem,
    g_send_sem,
    g_recv_sem,
    h_send_sem,
    h_recv_sem,
    x_send_sem,
    x_recv_sem,
    f_send_sem,
    f_recv_sem,
):
    g, t = lax.axis_index("grp"), lax.axis_index("tp")
    rows, positions = ck.shape[0], ck.shape[1]
    steps = nk_in.shape[1]
    heads = gain.shape[0]
    units, depth = wg32.shape
    per_key = heads // KVH
    per_col = heads // n_g
    halves = per_key // per_col
    height = steps * per_col
    inv_root = HD ** (-0.5)
    group_rows = rows * steps
    half_t = n_t // 2

    loads = [
        pltpu.make_async_copy(source, target, load_sem.at[i])
        for i, (source, target) in enumerate(
            (
                (q_hbm, q_in),
                (ck_hbm, ck),
                (cv_hbm, cv),
                (nk_hbm, nk_in),
                (nv_hbm, nv_in),
                (res_hbm, res_in),
                (gain_hbm, gain),
                (wg_hbm, wg32),
                (wd_hbm, wd32),
            )
        )
    ]
    for load in loads:
        load.start()

    peer_g = [g] + [lax.rem(g + k, n_g) for k in range(1, n_g)]
    peer_t = [t] + [lax.rem(t + k, n_t) for k in range(1, n_t)]
    far_first = sorted(range(n_t), key=lambda k: (k == 0, abs(k - half_t)))

    barrier = pltpu.get_barrier_semaphore()
    for peer in [(i, t) for i in peer_g[1:]] + [(g, k) for k in peer_t[1:]]:
        pl.semaphore_signal(barrier, inc=1, device_id=peer, device_id_type=MESH)

    def blocks_of(at):
        first = (at % 2) * n_t + at // 2
        return first, first + half_t

    mine = (lax.rem(t, 2) * n_t + t // 2, lax.rem(t, 2) * n_t + t // 2 + half_t)

    def by_block(source, target):
        flat = jnp.concatenate([source[r].astype(F32) for r in range(rows)], axis=0)
        for h in range(heads):
            target[h // per_col, pl.ds(h % per_col, group_rows, stride=per_col), :] = flat[
                :, h * HD : (h + 1) * HD
            ]

    loads[0].wait()
    by_block(q_in, q_rows)
    loads[1].wait()
    lane_place = t * positions + lax.broadcasted_iota(jnp.int32, (halves * height, positions), 1)
    pieces, shown = [], []
    tall = halves * height
    blank = jnp.zeros((tall, HD), F32)
    for r in range(rows):
        visible = (lane_place < lengths_ref[r]).astype(F32)
        query = []
        for j in range(KVH):
            own = jnp.concatenate(
                [
                    q_rows[j * halves + i, r * height : (r + 1) * height]
                    for i in range(halves)
                ],
                axis=0,
            )
            query.append(jnp.concatenate([blank] * j + [own] + [blank] * (KVH - 1 - j), axis=1))
            shown.append(visible)
        pieces.append(
            lax.dot_general(
                jnp.concatenate(query, axis=0).astype(BF16),
                ck[r],
                (((1,), (1,)), ((), ())),
                preferred_element_type=F32,
            )
        )
    shown = jnp.concatenate(shown, axis=0) > 0.0
    scores = jnp.where(shown, jnp.concatenate(pieces, axis=0) * inv_root, masked_score)
    highest = jnp.max(scores, axis=-1, keepdims=True)
    weights = jnp.where(shown, jnp.exp(scores - highest), 0.0)
    total = jnp.sum(weights, axis=-1, keepdims=True)
    weights = weights.astype(BF16)
    loads[2].wait()
    accum = []
    for r in range(rows):
        wide = jnp.dot(
            weights[r * KVH * tall : (r + 1) * KVH * tall], cv[r], preferred_element_type=F32
        )
        for j in range(KVH):
            accum.append(wide[j * tall : (j + 1) * tall, j * HD : (j + 1) * HD])
    some = total > 0.0
    safe = jnp.where(some, total, 1.0)
    means = jnp.concatenate(accum, axis=0) / safe
    logs = jnp.where(some, highest + jnp.log(safe), masked_score)

    def of_owner(array, at, i):
        b = blocks_of(at)[i]
        starts = [
            (r * KVH + b // halves) * tall + (b % halves) * height for r in range(rows)
        ]
        return jnp.concatenate([array[at : at + height] for at in starts], axis=0)

    block_rows = rows * height
    diagonal = lax.broadcasted_iota(jnp.int32, (block_rows, HD), 0) == lax.broadcasted_iota(
        jnp.int32, (block_rows, HD), 1
    )
    place = lax.broadcasted_iota(jnp.int32, (send_o.shape[2] - block_rows, HD), 0)

    def fill(at, i):
        lanes = jnp.sum(jnp.where(diagonal, of_owner(logs, at, i), 0.0), axis=0, keepdims=True)
        high = lanes.astype(BF16).astype(F32)
        middle = (lanes - high).astype(BF16).astype(F32)
        low = lanes - high - middle
        terms = jnp.where(place == 0, high, jnp.where(place == 1, middle, low))
        send_o[i, at] = jnp.concatenate([of_owner(means, at, i), terms], axis=0).astype(BF16)

    def along_tp(k, i, source, target, send_sem, recv_sem):
        return pltpu.make_async_remote_copy(
            src_ref=source.at[i, peer_t[k]],
            dst_ref=target.at[i, t],
            send_sem=send_sem.at[i * n_t + k],
            recv_sem=recv_sem.at[i * n_t + k],
            device_id=(g, peer_t[k]),
            device_id_type=MESH,
        )

    for i in range(2):
        for at in range(n_t):
            fill(at, i)
    pl.semaphore_wait(barrier, n_g + n_t - 2)
    row_copies = [
        [along_tp(k, i, send_o, recv_o, o_send_sem, o_recv_sem) for k in far_first[:-1]]
        for i in range(2)
    ]
    for i in range(2):
        for copy in row_copies[i]:
            copy.start()
        recv_o[i, t] = send_o[i, t]

    for load in loads[3:]:
        load.wait()
    by_block(res_in, res_rows)
    for source, target in ((nk_in, nk_rows), (nv_in, nv_rows)):
        flat = jnp.concatenate([source[r].astype(F32) for r in range(rows)], axis=0)
        for j in range(KVH):
            target[j] = flat[:, j * HD : (j + 1) * HD]

    def new_tokens(tokens, at, b):
        held = tokens[b // halves]
        return jnp.concatenate(
            [
                jnp.broadcast_to(held[r * steps + at : r * steps + at + 1], (height, HD))
                for r in range(rows)
            ],
            axis=0,
        )

    step_of = lax.broadcasted_iota(jnp.int32, (block_rows, 1), 0) & (height - 1)
    seen = [step_of >= at * per_col for at in range(steps)]
    fresh = [
        [
            jnp.where(
                seen[at],
                jnp.sum(q_rows[b] * new_tokens(nk_rows, at, b), axis=-1, keepdims=True)
                * inv_root,
                masked_score,
            )
            for at in range(steps)
        ]
        for b in mine
    ]
    new_held = [[new_tokens(nv_rows, at, b) for at in range(steps)] for b in mine]
    spare = jnp.zeros((wg.shape[0] - units, depth), F32)
    wg[...] = jnp.concatenate([wg32[...], spare], axis=0).astype(BF16)
    wd[...] = jnp.concatenate([wd32[...], spare], axis=0).astype(BF16)

    def finish_context(i):
        logs = []
        for at in range(n_t):
            terms = recv_o[i, at, block_rows:].astype(F32)
            lanes = terms[0:1] + terms[1:2] + terms[2:3]
            logs.append(jnp.sum(jnp.where(diagonal, lanes, 0.0), axis=-1, keepdims=True))
        joint = functools.reduce(jnp.maximum, logs + fresh[i])
        total, accum = 0.0, 0.0
        for at in range(n_t):
            weight = jnp.exp(logs[at] - joint)
            total = total + weight
            accum = accum + weight * recv_o[i, at, :block_rows].astype(F32)
        for at in range(steps):
            weight = jnp.where(seen[at], jnp.exp(fresh[i][at] - joint), 0.0)
            total = total + weight
            accum = accum + weight.astype(BF16).astype(F32) * new_held[i][at]
        send_x[i] = (res_rows[mine[i]] + accum / total).astype(BF16)

    class Spread:
        def __init__(self, source, target, send_sem, recv_sem):
            self.refs = source, target, send_sem, recv_sem

        def each(self, action, parts):
            source, target, send_sem, recv_sem = self.refs
            for i in parts:
                for k in far_first:
                    copy = pltpu.make_async_remote_copy(
                        src_ref=source.at[i],
                        dst_ref=target(g),
                        send_sem=send_sem.at[i * n_t + k],
                        recv_sem=recv_sem.at[g],
                        device_id=(mine[i], peer_t[k]),
                        device_id_type=MESH,
                    )
                    if k:
                        action(copy)
                    else:
                        pl.when(mine[i] != g)(functools.partial(action, copy))

        def start(self, i):
            self.each(lambda copy: copy.start(), (i,))
            source, target, _, recv_sem = self.refs
            here = pltpu.make_async_copy(source.at[i], target(g), recv_sem.at[g])
            pl.when(mine[i] == g)(here.start)

        def wait_send(self):
            self.each(lambda copy: copy.wait_send(), range(2))

        def wait_recv(self, parts):
            source, target, _, recv_sem = self.refs
            for i in parts:
                pltpu.make_async_copy(source.at[0], target(i), recv_sem.at[i]).wait()

    x_spread = Spread(send_x, lambda i: recv_x.at[i], x_send_sem, x_recv_sem)
    for i in range(2):
        for copy in row_copies[i]:
            copy.wait_recv()
        finish_context(i)
        x_spread.start(i)

    parts = [[blocks_of(at)[i] for at in range(n_t)] for i in range(2)]
    part_rows = n_t * group_rows
    gains = [gain[pl.ds(g * per_col + c, 1)] for c in range(per_col)]

    def part_gate(i):
        x_spread.wait_recv(parts[i])
        x_rows[i] = jnp.concatenate([recv_x[b].astype(F32) for b in parts[i]], axis=0)
        columns = [
            x_rows.at[i][pl.ds(c, part_rows, stride=per_col), :] for c in range(per_col)
        ]
        squares = jnp.sum(
            functools.reduce(jnp.add, [c * c for c in columns]), axis=-1, keepdims=True
        )
        scaled = jnp.concatenate([c * by for c, by in zip(columns, gains)], axis=1).astype(BF16)
        gate = lax.dot_general(
            scaled, wg[...], (((1,), (1,)), ((), ())), preferred_element_type=F32
        )
        spare_lane = lax.broadcasted_iota(jnp.int32, gate.shape, 1) >= units
        gate = jnp.where(spare_lane, squares, gate)
        for at, b in enumerate(parts[i]):
            send_g[b] = gate[at * group_rows : (at + 1) * group_rows].astype(BF16)
        return columns

    def along_grp(k, source, target, send_sem, recv_sem):
        return pltpu.make_async_remote_copy(
            src_ref=source,
            dst_ref=target.at[g],
            send_sem=send_sem.at[k - 1],
            recv_sem=recv_sem.at[k - 1],
            device_id=(peer_g[k], t),
            device_id_type=MESH,
        )

    gate_copies = [
        along_grp(k, send_g.at[peer_g[k]], recv_g, g_send_sem, g_recv_sem) for k in range(1, n_g)
    ]
    for i in range(2):
        columns = part_gate(i)
        for k in range(1, n_g):
            in_part = functools.reduce(jnp.logical_or, [peer_g[k] == b for b in parts[i]])
            pl.when(in_part)(gate_copies[k - 1].start)
        wide = jnp.concatenate(columns, axis=1)
        for at, b in enumerate(parts[i]):
            x_flat[b] = wide[at * group_rows : (at + 1) * group_rows]
    recv_g[g] = send_g[g]
    for copy in gate_copies:
        copy.wait_recv()
    whole = functools.reduce(jnp.add, [recv_g[i].astype(F32) for i in range(n_g)])
    square = whole[:, units : units + 1]
    whole = whole * lax.rsqrt(square / (heads * HD) + 1e-05)
    own_hidden = (whole / (1.0 + jnp.exp(-whole))).astype(BF16)

    send_h[...] = own_hidden
    hidden_copies = [
        pltpu.make_async_remote_copy(
            src_ref=send_h,
            dst_ref=recv_h.at[g],
            send_sem=h_send_sem.at[k],
            recv_sem=h_recv_sem.at[g],
            device_id=(peer_g[k], t),
            device_id_type=MESH,
        )
        for k in range(1, n_g)
    ]
    for copy in hidden_copies:
        copy.start()
    pltpu.make_async_copy(send_h, recv_h.at[g], h_recv_sem.at[g]).start()

    mlp_copies = [
        [along_tp(k, i, send_m, recv_m, m_send_sem, m_recv_sem) for k in far_first[:-1]]
        for i in range(2)
    ]
    for i in range(2):
        for b in parts[i]:
            pltpu.make_async_copy(send_h, recv_h.at[b], h_recv_sem.at[b]).wait()
        hidden = jnp.concatenate([recv_h[b].astype(F32) for b in parts[i]], axis=0).astype(BF16)
        mlp = jnp.dot(hidden, wd[...], preferred_element_type=F32)
        for at in range(n_t):
            send_m[i, at] = mlp[at * group_rows : (at + 1) * group_rows].astype(BF16)
        for copy in mlp_copies[i]:
            copy.start()
        recv_m[i, t] = send_m[i, t]

    def out_columns(i):
        return out_ref.at[:, :, pl.ds(pl.multiple_of(i * depth, depth), depth)]

    f_spread = Spread(send_f, out_columns, f_send_sem, f_recv_sem)
    for i in range(2):
        for copy in mlp_copies[i]:
            copy.wait_recv()
        done = functools.reduce(jnp.add, [recv_m[i, at].astype(F32) for at in range(n_t)])
        done = (x_flat[mine[i]] + done).astype(BF16)
        for r in range(rows):
            send_f[i, r] = done[r * steps : (r + 1) * steps]
        f_spread.start(i)
    for copy in row_copies[0] + row_copies[1] + gate_copies + hidden_copies:
        copy.wait_send()
    for copy in mlp_copies[0] + mlp_copies[1]:
        copy.wait_send()
    x_spread.wait_send()
    f_spread.wait_recv(range(n_g))
    f_spread.wait_send()


def moved_activations(
    n_g,
    n_t,
    queries,
    cache_keys,
    cache_values,
    new_keys,
    new_values,
    lengths,
    residual,
    norm_gain,
    w_gate,
    w_down,
):
    rows, steps, features = queries.shape
    positions, kv_width = cache_keys.shape[1:]
    depth, units = w_gate.shape
    heads = features // HD
    per_col = heads // n_g
    height = steps * per_col
    group_rows = rows * steps
    wide = (units // HD + 1) * HD
    hbm = pl.BlockSpec(memory_space=pltpu.HBM)
    dma = pltpu.SemaphoreType.DMA
    return pl.pallas_call(
        functools.partial(layer_kernel, n_g, n_t),
        out_shape=jax.ShapeDtypeStruct(queries.shape, BF16),
        in_specs=[pl.BlockSpec(memory_space=pltpu.SMEM)] + [hbm] * 9,
        out_specs=hbm,
        scratch_shapes=[
            pltpu.VMEM(queries.shape, BF16),
            pltpu.VMEM(new_keys.shape, BF16),
            pltpu.VMEM(new_values.shape, BF16),
            pltpu.VMEM(residual.shape, BF16),
            pltpu.VMEM((heads, HD), F32),
            pltpu.VMEM(cache_keys.shape, BF16),
            pltpu.VMEM(cache_values.shape, BF16),
            pltpu.VMEM((units, depth), F32),
            pltpu.VMEM((units, depth), F32),
            pltpu.VMEM((wide, depth), BF16),
            pltpu.VMEM((wide, depth), BF16),
            pltpu.VMEM((n_g, rows * height, HD), F32),
            pltpu.VMEM((n_g, rows * height, HD), F32),
            pltpu.VMEM((KVH, group_rows, HD), F32),
            pltpu.VMEM((KVH, group_rows, HD), F32),
            pltpu.VMEM((2, n_t, rows * height + 16, HD), BF16),
            pltpu.VMEM((2, n_t, rows * height + 16, HD), BF16),
            pltpu.VMEM((2, rows * height, HD), BF16),
            pltpu.VMEM((n_g, rows * height, HD), BF16),
            pltpu.VMEM((2, n_t * rows * height, HD), F32),
            pltpu.VMEM((n_g, group_rows, depth), F32),
            pltpu.VMEM((n_g, group_rows, wide), BF16),
            pltpu.VMEM((n_g, group_rows, wide), BF16),
            pltpu.VMEM((group_rows, wide), BF16),
            pltpu.VMEM((n_g, group_rows, wide), BF16),
            pltpu.VMEM((2, n_t, group_rows, depth), BF16),
            pltpu.VMEM((2, n_t, group_rows, depth), BF16),
            pltpu.VMEM((2, rows, steps, depth), BF16),
            dma((9,)),
        ]
        + [dma((2 * n_t,))] * 4
        + [dma((n_g,))] * 8,
        compiler_params=pltpu.CompilerParams(
            collective_id=0, has_side_effects=True, vmem_limit_bytes=56 * 1024 * 1024
        ),
    )(
        lengths,
        queries,
        new_keys,
        new_values,
        residual,
        norm_gain.reshape(heads, HD),
        cache_keys,
        cache_values,
        w_gate.T,
        w_down.T,
    )


def shards(n_g, n_t, *arrays):
    queries, cache_keys = arrays[0], arrays[1]
    rows, steps, features = queries.shape
    heads = features // HD
    kv_heads = cache_keys.shape[2] // HD
    even = (
        n_g == 2 * n_t
        and n_t % 2 == 0
        and heads % n_g == 0
        and n_g % kv_heads == 0
        and steps * (heads // n_g) == 8
        and rows * steps == 8
    )
    if even:
        return moved_activations(n_g, n_t, *arrays)
    return gathered_weights(*arrays)


def solution(mesh):
    return jax.shard_map(
        functools.partial(shards, mesh.shape["grp"], mesh.shape["tp"]),
        mesh=mesh,
        in_specs=(
            P("grp", None, None),
            P("grp", "tp", None),
            P("grp", "tp", None),
            P("grp", None, None),
            P("grp", None, None),
            P("grp"),
            P("grp", None, None),
            P(),
            P("grp", "tp"),
            P("grp", "tp"),
        ),
        out_specs=P("grp", None, None),
        check_vma=False,
    )
```

```python
import functools

import jax
import jax.numpy as jnp
from jax import lax
from jax.experimental import pallas as pl
from jax.experimental.pallas import tpu as pltpu
from jax.sharding import PartitionSpec as P

HD = 128
KVH = 4


masked_score = -1e30


def merged_2(shard, axis, join):
    gathered = jax.tree.map(
        lambda a, kind: lax.all_gather(a.astype(kind), axis),
        shard,
        jax.tree.map(lambda a: jnp.bfloat16 if a.dtype == jnp.float32 else a.dtype, shard),
    )

    def take(source):
        return jax.tree.map(
            lambda a, own: lax.dynamic_index_in_dim(a, source, 0, False).astype(own.dtype),
            gathered,
            shard,
        )

    return lax.fori_loop(
        1, lax.axis_size(axis), lambda source, state: join(state, take(source)), take(0)
    )


def combine_parts(earlier, later):
    first_max, first_total, first_accum = earlier
    second_max, second_total, second_accum = later
    joint_max = jnp.maximum(first_max, second_max)
    first_factor = jnp.exp(first_max - joint_max)
    second_factor = jnp.exp(second_max - joint_max)
    joint_total = first_total * first_factor + second_total * second_factor
    joint_accum = first_accum * first_factor[..., None] + second_accum * second_factor[..., None]
    return (joint_max, joint_total, joint_accum)


def partial_softmax(scores, visible, value_heads, formula):
    scores = jnp.where(visible, scores, masked_score)
    highest = jnp.max(scores, axis=-1)
    weights = jnp.where(visible, jnp.exp(scores - highest[..., None]), 0.0)
    totals = jnp.sum(weights, axis=-1)
    accum = jnp.einsum(
        formula, weights.astype(jnp.bfloat16), value_heads, preferred_element_type=jnp.float32
    )
    return (highest, totals, accum)


def gathered_weights(
    queries,
    cache_keys,
    cache_values,
    new_keys,
    new_values,
    lengths,
    residual,
    norm_gain,
    w_gate,
    w_down,
):
    row_count, step_count, features = queries.shape
    positions = cache_keys.shape[1]
    per_group = features // (KVH * HD)
    inv_root = HD ** (-0.5)
    query_heads = queries.reshape(row_count, step_count, KVH, per_group, HD)
    key_heads = cache_keys.reshape(row_count, positions, KVH, HD)
    value_heads = cache_values.reshape(row_count, positions, KVH, HD)
    cached_scores = (
        jnp.einsum("rsjgd,rcjd->rsjgc", query_heads, key_heads, preferred_element_type=jnp.float32)
        * inv_root
    )
    offset = lax.axis_index("tp") * positions
    places = offset + lax.broadcasted_iota(jnp.int32, (row_count, positions), 1)
    visible = (places < lengths[:, None])[:, None, None, None, :]
    local_part = partial_softmax(cached_scores, visible, value_heads, "rsjgc,rcjd->rsjgd")
    merged = merged_2(local_part, "tp", combine_parts)
    fresh_key_heads = new_keys.reshape(row_count, step_count, KVH, HD)
    fresh_value_heads = new_values.reshape(row_count, step_count, KVH, HD)
    fresh_scores = (
        jnp.einsum(
            "rsjgd,rtjd->rsjgt", query_heads, fresh_key_heads, preferred_element_type=jnp.float32
        )
        * inv_root
    )
    causal = lax.broadcasted_iota(jnp.int32, (step_count, step_count), 0) >= lax.broadcasted_iota(
        jnp.int32, (step_count, step_count), 1
    )
    causal = causal[None, :, None, None, :]
    fresh_part = partial_softmax(fresh_scores, causal, fresh_value_heads, "rsjgt,rtjd->rsjgd")
    joint_max, joint_total, joint_accum = combine_parts(merged, fresh_part)
    context = (joint_accum / joint_total[..., None]).reshape(row_count, step_count, features)
    summed = residual.astype(jnp.float32) + context
    mean_square = jnp.mean(summed * summed, axis=-1, keepdims=True)
    normed = (summed * lax.rsqrt(mean_square + 1e-05) * norm_gain).astype(jnp.bfloat16)
    flat = normed.reshape(row_count * step_count, features)
    gate_policy, down_policy = (
        lax.all_gather(w_gate.astype(jnp.bfloat16), "grp", axis=0, tiled=True),
        lax.all_gather(w_down.astype(jnp.bfloat16), "grp", axis=0, tiled=True),
    )
    gate = jnp.dot(flat, gate_policy, preferred_element_type=jnp.float32)
    hidden = jax.nn.silu(gate).astype(jnp.bfloat16)
    partial_sum = lax.dot_general(
        hidden, down_policy, (((1,), (1,)), ((), ())), preferred_element_type=jnp.float32
    )
    mlp = lax.psum(partial_sum.astype(jnp.bfloat16), "tp").astype(jnp.float32)
    return (summed + mlp.reshape(row_count, step_count, features)).astype(jnp.bfloat16)


MESH = pl.DeviceIdType.MESH
BF16, F32 = jnp.bfloat16, jnp.float32


def layer_kernel(
    n_g,
    n_t,
    lengths_hbm,
    q_hbm,
    nk_hbm,
    nv_hbm,
    res_hbm,
    gain_hbm,
    ck_hbm,
    cv_hbm,
    wg_hbm,
    wd_hbm,
    out_ref,
    lengths_ref,
    q_in,
    nk_in,
    nv_in,
    res_in,
    gain,
    ck,
    cv,
    wg32,
    wd32,
    wg,
    wd,
    q_rows,
    res_rows,
    nk_rows,
    nv_rows,
    send_o,
    recv_o,
    send_x,
    recv_x,
    x_rows,
    x_flat,
    send_g,
    recv_g,
    send_h,
    recv_h,
    send_m,
    recv_m,
    send_f,
    load_sem,
    o_send_sem,
    o_recv_sem,
    m_send_sem,
    m_recv_sem,
    g_send_sem,
    g_recv_sem,
    h_send_sem,
    h_recv_sem,
    x_send_sem,
    x_recv_sem,
    f_send_sem,
    f_recv_sem,
):
    g, t = lax.axis_index("grp"), lax.axis_index("tp")
    rows, positions = ck.shape[0], ck.shape[1]
    steps = nk_in.shape[1]
    heads = gain.shape[0]
    units, depth = wg32.shape
    per_key = heads // KVH
    per_col = heads // n_g
    halves = per_key // per_col
    height = steps * per_col
    inv_root = HD ** (-0.5)
    group_rows = rows * steps
    half_t = n_t // 2

    peer_g = [g] + [lax.rem(g + k, n_g) for k in range(1, n_g)]
    peer_t = [t] + [lax.rem(t + k, n_t) for k in range(1, n_t)]
    far_first = sorted(range(n_t), key=lambda k: (k == 0, abs(k - half_t)))

    barrier = pltpu.get_barrier_semaphore()
    for peer in [(i, t) for i in peer_g[1:]] + [(g, k) for k in peer_t[1:]]:
        pl.semaphore_signal(barrier, inc=1, device_id=peer, device_id_type=MESH)

    loads = [
        pltpu.make_async_copy(source, target, load_sem.at[i])
        for i, (source, target) in enumerate(
            (
                (q_hbm, q_in),
                (lengths_hbm, lengths_ref),
                (ck_hbm, ck),
                (cv_hbm, cv),
                (nk_hbm, nk_in),
                (nv_hbm, nv_in),
                (res_hbm, res_in),
                (gain_hbm, gain),
                (wg_hbm, wg32),
                (wd_hbm, wd32),
            )
        )
    ]
    for load in loads:
        load.start()

    def blocks_of(at):
        first = (at % 2) * n_t + at // 2
        return first, first + half_t

    mine = (lax.rem(t, 2) * n_t + t // 2, lax.rem(t, 2) * n_t + t // 2 + half_t)

    def by_block(source, target):
        flat = jnp.concatenate([source[r].astype(F32) for r in range(rows)], axis=0)
        for h in range(heads):
            target[h // per_col, pl.ds(h % per_col, group_rows, stride=per_col), :] = flat[
                :, h * HD : (h + 1) * HD
            ]

    loads[0].wait()
    by_block(q_in, q_rows)
    loads[1].wait()
    loads[2].wait()
    lane_place = t * positions + lax.broadcasted_iota(jnp.int32, (halves * height, positions), 1)
    pieces, shown = [], []
    tall = halves * height
    blank = jnp.zeros((tall, HD), F32)
    for r in range(rows):
        visible = (lane_place < lengths_ref[r]).astype(F32)
        query = []
        for j in range(KVH):
            own = jnp.concatenate(
                [
                    q_rows[j * halves + i, r * height : (r + 1) * height]
                    for i in range(halves)
                ],
                axis=0,
            )
            query.append(jnp.concatenate([blank] * j + [own] + [blank] * (KVH - 1 - j), axis=1))
            shown.append(visible)
        pieces.append(
            lax.dot_general(
                jnp.concatenate(query, axis=0).astype(BF16),
                ck[r],
                (((1,), (1,)), ((), ())),
                preferred_element_type=F32,
            )
        )
    shown = jnp.concatenate(shown, axis=0) > 0.0
    scores = jnp.where(shown, jnp.concatenate(pieces, axis=0) * inv_root, masked_score)
    highest = jnp.max(scores, axis=-1, keepdims=True)
    weights = jnp.where(shown, jnp.exp(scores - highest), 0.0)
    total = jnp.sum(weights, axis=-1, keepdims=True)
    weights = weights.astype(BF16)
    loads[3].wait()
    accum = []
    for r in range(rows):
        wide = jnp.dot(
            weights[r * KVH * tall : (r + 1) * KVH * tall], cv[r], preferred_element_type=F32
        )
        for j in range(KVH):
            accum.append(wide[j * tall : (j + 1) * tall, j * HD : (j + 1) * HD])
    some = total > 0.0
    safe = jnp.where(some, total, 1.0)
    means = jnp.concatenate(accum, axis=0) / safe
    logs = jnp.where(some, highest + jnp.log(safe), masked_score)

    def of_owner(array, at, i):
        b = blocks_of(at)[i]
        starts = [
            (r * KVH + b // halves) * tall + (b % halves) * height for r in range(rows)
        ]
        return jnp.concatenate([array[at : at + height] for at in starts], axis=0)

    block_rows = rows * height
    diagonal = lax.broadcasted_iota(jnp.int32, (block_rows, HD), 0) == lax.broadcasted_iota(
        jnp.int32, (block_rows, HD), 1
    )
    place = lax.broadcasted_iota(jnp.int32, (send_o.shape[2] - block_rows, HD), 0)

    def fill(at, i):
        lanes = jnp.sum(jnp.where(diagonal, of_owner(logs, at, i), 0.0), axis=0, keepdims=True)
        high = lanes.astype(BF16).astype(F32)
        middle = (lanes - high).astype(BF16).astype(F32)
        low = lanes - high - middle
        terms = jnp.where(place == 0, high, jnp.where(place == 1, middle, low))
        send_o[i, at] = jnp.concatenate([of_owner(means, at, i), terms], axis=0).astype(BF16)

    def along_tp(k, i, source, target, send_sem, recv_sem):
        return pltpu.make_async_remote_copy(
            src_ref=source.at[i, peer_t[k]],
            dst_ref=target.at[i, t],
            send_sem=send_sem.at[i * n_t + k],
            recv_sem=recv_sem.at[i * n_t + k],
            device_id=(g, peer_t[k]),
            device_id_type=MESH,
        )

    for i in range(2):
        for at in range(n_t):
            fill(at, i)
    pl.semaphore_wait(barrier, n_g + n_t - 2)
    row_copies = [
        [along_tp(k, i, send_o, recv_o, o_send_sem, o_recv_sem) for k in far_first[:-1]]
        for i in range(2)
    ]
    for i in range(2):
        for copy in row_copies[i]:
            copy.start()
        recv_o[i, t] = send_o[i, t]

    for load in loads[4:8]:
        load.wait()
    by_block(res_in, res_rows)
    for source, target in ((nk_in, nk_rows), (nv_in, nv_rows)):
        flat = jnp.concatenate([source[r].astype(F32) for r in range(rows)], axis=0)
        for j in range(KVH):
            target[j] = flat[:, j * HD : (j + 1) * HD]

    def new_tokens(tokens, at, b):
        held = tokens[b // halves]
        return jnp.concatenate(
            [
                jnp.broadcast_to(held[r * steps + at : r * steps + at + 1], (height, HD))
                for r in range(rows)
            ],
            axis=0,
        )

    step_of = lax.broadcasted_iota(jnp.int32, (block_rows, 1), 0) & (height - 1)
    seen = [step_of >= at * per_col for at in range(steps)]
    fresh = [
        [
            jnp.where(
                seen[at],
                jnp.sum(q_rows[b] * new_tokens(nk_rows, at, b), axis=-1, keepdims=True)
                * inv_root,
                masked_score,
            )
            for at in range(steps)
        ]
        for b in mine
    ]
    new_held = [[new_tokens(nv_rows, at, b) for at in range(steps)] for b in mine]
    loads[8].wait()
    spare = jnp.zeros((wg.shape[0] - units, depth), F32)
    wg[...] = jnp.concatenate([wg32[...], spare], axis=0).astype(BF16)

    def finish_context(i):
        logs = []
        for at in range(n_t):
            terms = recv_o[i, at, block_rows:].astype(F32)
            lanes = terms[0:1] + terms[1:2] + terms[2:3]
            logs.append(jnp.sum(jnp.where(diagonal, lanes, 0.0), axis=-1, keepdims=True))
        joint = functools.reduce(jnp.maximum, logs + fresh[i])
        total, accum = 0.0, 0.0
        for at in range(n_t):
            weight = jnp.exp(logs[at] - joint)
            total = total + weight
            accum = accum + weight * recv_o[i, at, :block_rows].astype(F32)
        for at in range(steps):
            weight = jnp.where(seen[at], jnp.exp(fresh[i][at] - joint), 0.0)
            total = total + weight
            accum = accum + weight.astype(BF16).astype(F32) * new_held[i][at]
        send_x[i] = (res_rows[mine[i]] + accum / total).astype(BF16)

    class Spread:
        def __init__(self, source, target, send_sem, recv_sem):
            self.refs = source, target, send_sem, recv_sem

        def each(self, action, parts):
            source, target, send_sem, recv_sem = self.refs
            for i in parts:
                for k in far_first:
                    copy = pltpu.make_async_remote_copy(
                        src_ref=source.at[i],
                        dst_ref=target(g),
                        send_sem=send_sem.at[i * n_t + k],
                        recv_sem=recv_sem.at[g],
                        device_id=(mine[i], peer_t[k]),
                        device_id_type=MESH,
                    )
                    if k:
                        action(copy)
                    else:
                        pl.when(mine[i] != g)(functools.partial(action, copy))

        def start(self, i):
            self.each(lambda copy: copy.start(), (i,))
            source, target, _, recv_sem = self.refs
            here = pltpu.make_async_copy(source.at[i], target(g), recv_sem.at[g])
            pl.when(mine[i] == g)(here.start)

        def wait_send(self):
            self.each(lambda copy: copy.wait_send(), range(2))

        def wait_recv(self, parts):
            source, target, _, recv_sem = self.refs
            for i in parts:
                pltpu.make_async_copy(source.at[0], target(i), recv_sem.at[i]).wait()

    x_spread = Spread(send_x, lambda i: recv_x.at[i], x_send_sem, x_recv_sem)
    for i in range(2):
        for copy in row_copies[i]:
            copy.wait_recv()
        finish_context(i)
        x_spread.start(i)

    parts = [[blocks_of(at)[i] for at in range(n_t)] for i in range(2)]
    part_rows = n_t * group_rows
    gains = [gain[pl.ds(g * per_col + c, 1)] for c in range(per_col)]

    def part_gate(i):
        x_spread.wait_recv(parts[i])
        x_rows[i] = jnp.concatenate([recv_x[b].astype(F32) for b in parts[i]], axis=0)
        columns = [
            x_rows.at[i][pl.ds(c, part_rows, stride=per_col), :] for c in range(per_col)
        ]
        squares = jnp.sum(
            functools.reduce(jnp.add, [c * c for c in columns]), axis=-1, keepdims=True
        )
        scaled = jnp.concatenate([c * by for c, by in zip(columns, gains)], axis=1).astype(BF16)
        gate = lax.dot_general(
            scaled, wg[...], (((1,), (1,)), ((), ())), preferred_element_type=F32
        )
        spare_lane = lax.broadcasted_iota(jnp.int32, gate.shape, 1) >= units
        gate = jnp.where(spare_lane, squares, gate)
        for at, b in enumerate(parts[i]):
            send_g[b] = gate[at * group_rows : (at + 1) * group_rows].astype(BF16)
        return columns

    def along_grp(k, source, target, send_sem, recv_sem):
        return pltpu.make_async_remote_copy(
            src_ref=source,
            dst_ref=target.at[g],
            send_sem=send_sem.at[k - 1],
            recv_sem=recv_sem.at[k - 1],
            device_id=(peer_g[k], t),
            device_id_type=MESH,
        )

    gate_copies = [
        along_grp(k, send_g.at[peer_g[k]], recv_g, g_send_sem, g_recv_sem) for k in range(1, n_g)
    ]
    for i in range(2):
        columns = part_gate(i)
        for k in range(1, n_g):
            in_part = functools.reduce(jnp.logical_or, [peer_g[k] == b for b in parts[i]])
            pl.when(in_part)(gate_copies[k - 1].start)
        wide = jnp.concatenate(columns, axis=1)
        for at, b in enumerate(parts[i]):
            x_flat[b] = wide[at * group_rows : (at + 1) * group_rows]
    recv_g[g] = send_g[g]
    loads[9].wait()
    wd[...] = jnp.concatenate([wd32[...], spare], axis=0).astype(BF16)
    for copy in gate_copies:
        copy.wait_recv()
    whole = functools.reduce(jnp.add, [recv_g[i].astype(F32) for i in range(n_g)])
    square = whole[:, units : units + 1]
    whole = whole * lax.rsqrt(square / (heads * HD) + 1e-05)
    own_hidden = (whole / (1.0 + jnp.exp(-whole))).astype(BF16)

    send_h[...] = own_hidden
    hidden_copies = [
        pltpu.make_async_remote_copy(
            src_ref=send_h,
            dst_ref=recv_h.at[g],
            send_sem=h_send_sem.at[k],
            recv_sem=h_recv_sem.at[g],
            device_id=(peer_g[k], t),
            device_id_type=MESH,
        )
        for k in range(1, n_g)
    ]
    for copy in hidden_copies:
        copy.start()
    pltpu.make_async_copy(send_h, recv_h.at[g], h_recv_sem.at[g]).start()

    mlp_copies = [
        [along_tp(k, i, send_m, recv_m, m_send_sem, m_recv_sem) for k in far_first[:-1]]
        for i in range(2)
    ]
    for i in range(2):
        for b in parts[i]:
            pltpu.make_async_copy(send_h, recv_h.at[b], h_recv_sem.at[b]).wait()
        hidden = jnp.concatenate([recv_h[b].astype(F32) for b in parts[i]], axis=0).astype(BF16)
        mlp = jnp.dot(hidden, wd[...], preferred_element_type=F32)
        for at in range(n_t):
            send_m[i, at] = mlp[at * group_rows : (at + 1) * group_rows].astype(BF16)
        for copy in mlp_copies[i]:
            copy.start()
        recv_m[i, t] = send_m[i, t]

    def out_columns(i):
        return out_ref.at[:, :, pl.ds(pl.multiple_of(i * depth, depth), depth)]

    f_spread = Spread(send_f, out_columns, f_send_sem, f_recv_sem)
    for i in range(2):
        for copy in mlp_copies[i]:
            copy.wait_recv()
        done = functools.reduce(jnp.add, [recv_m[i, at].astype(F32) for at in range(n_t)])
        done = (x_flat[mine[i]] + done).astype(BF16)
        for r in range(rows):
            send_f[i, r] = done[r * steps : (r + 1) * steps]
        f_spread.start(i)
    for copy in row_copies[0] + row_copies[1] + gate_copies + hidden_copies:
        copy.wait_send()
    for copy in mlp_copies[0] + mlp_copies[1]:
        copy.wait_send()
    x_spread.wait_send()
    f_spread.wait_recv(range(n_g))
    f_spread.wait_send()


def moved_activations(
    n_g,
    n_t,
    queries,
    cache_keys,
    cache_values,
    new_keys,
    new_values,
    lengths,
    residual,
    norm_gain,
    w_gate,
    w_down,
):
    rows, steps, features = queries.shape
    positions, kv_width = cache_keys.shape[1:]
    depth, units = w_gate.shape
    heads = features // HD
    per_col = heads // n_g
    height = steps * per_col
    group_rows = rows * steps
    wide = (units // HD + 1) * HD
    hbm = pl.BlockSpec(memory_space=pltpu.HBM)
    dma = pltpu.SemaphoreType.DMA
    return pl.pallas_call(
        functools.partial(layer_kernel, n_g, n_t),
        out_shape=pltpu.VMEM(queries.shape, BF16),
        in_specs=[hbm] * 10,
        out_specs=pl.BlockSpec(memory_space=pltpu.VMEM),
        scratch_shapes=[
            pltpu.SMEM(lengths.shape, jnp.int32),
            pltpu.VMEM(queries.shape, BF16),
            pltpu.VMEM(new_keys.shape, BF16),
            pltpu.VMEM(new_values.shape, BF16),
            pltpu.VMEM(residual.shape, BF16),
            pltpu.VMEM((heads, HD), F32),
            pltpu.VMEM(cache_keys.shape, BF16),
            pltpu.VMEM(cache_values.shape, BF16),
            pltpu.VMEM((units, depth), F32),
            pltpu.VMEM((units, depth), F32),
            pltpu.VMEM((wide, depth), BF16),
            pltpu.VMEM((wide, depth), BF16),
            pltpu.VMEM((n_g, rows * height, HD), F32),
            pltpu.VMEM((n_g, rows * height, HD), F32),
            pltpu.VMEM((KVH, group_rows, HD), F32),
            pltpu.VMEM((KVH, group_rows, HD), F32),
            pltpu.VMEM((2, n_t, rows * height + 16, HD), BF16),
            pltpu.VMEM((2, n_t, rows * height + 16, HD), BF16),
            pltpu.VMEM((2, rows * height, HD), BF16),
            pltpu.VMEM((n_g, rows * height, HD), BF16),
            pltpu.VMEM((2, n_t * rows * height, HD), F32),
            pltpu.VMEM((n_g, group_rows, depth), F32),
            pltpu.VMEM((n_g, group_rows, wide), BF16),
            pltpu.VMEM((n_g, group_rows, wide), BF16),
            pltpu.VMEM((group_rows, wide), BF16),
            pltpu.VMEM((n_g, group_rows, wide), BF16),
            pltpu.VMEM((2, n_t, group_rows, depth), BF16),
            pltpu.VMEM((2, n_t, group_rows, depth), BF16),
            pltpu.VMEM((2, rows, steps, depth), BF16),
            dma((10,)),
        ]
        + [dma((2 * n_t,))] * 4
        + [dma((n_g,))] * 8,
        compiler_params=pltpu.CompilerParams(
            collective_id=0, has_side_effects=True, vmem_limit_bytes=40 * 1024 * 1024
        ),
    )(
        *(
            pltpu.with_memory_space_constraint(array, pltpu.HBM)
            for array in (
                lengths,
                queries,
                new_keys,
                new_values,
                residual,
                norm_gain.reshape(heads, HD),
                cache_keys,
                cache_values,
                w_gate.T,
                w_down.T,
            )
        ),
    )


def shards(n_g, n_t, *arrays):
    queries, cache_keys = arrays[0], arrays[1]
    rows, steps, features = queries.shape
    heads = features // HD
    kv_heads = cache_keys.shape[2] // HD
    even = (
        n_g == 2 * n_t
        and n_t % 2 == 0
        and heads % n_g == 0
        and n_g % kv_heads == 0
        and steps * (heads // n_g) == 8
        and rows * steps == 8
    )
    if even:
        return moved_activations(n_g, n_t, *arrays)
    return gathered_weights(*arrays)


def solution(mesh):
    return jax.shard_map(
        functools.partial(shards, mesh.shape["grp"], mesh.shape["tp"]),
        mesh=mesh,
        in_specs=(
            P("grp", None, None),
            P("grp", "tp", None),
            P("grp", "tp", None),
            P("grp", None, None),
            P("grp", None, None),
            P("grp"),
            P("grp", None, None),
            P(),
            P("grp", "tp"),
            P("grp", "tp"),
        ),
        out_specs=P("grp", None, None),
        check_vma=False,
    )
```

```python
import functools

import jax
import jax.numpy as jnp
from jax import lax
from jax.experimental import pallas as pl
from jax.experimental.pallas import tpu as pltpu
from jax.sharding import PartitionSpec as P

HD = 128
KVH = 4


masked_score = -1e30


def merged_2(shard, axis, join):
    gathered = jax.tree.map(
        lambda a, kind: lax.all_gather(a.astype(kind), axis),
        shard,
        jax.tree.map(lambda a: jnp.bfloat16 if a.dtype == jnp.float32 else a.dtype, shard),
    )

    def take(source):
        return jax.tree.map(
            lambda a, own: lax.dynamic_index_in_dim(a, source, 0, False).astype(own.dtype),
            gathered,
            shard,
        )

    return lax.fori_loop(
        1, lax.axis_size(axis), lambda source, state: join(state, take(source)), take(0)
    )


def combine_parts(earlier, later):
    first_max, first_total, first_accum = earlier
    second_max, second_total, second_accum = later
    joint_max = jnp.maximum(first_max, second_max)
    first_factor = jnp.exp(first_max - joint_max)
    second_factor = jnp.exp(second_max - joint_max)
    joint_total = first_total * first_factor + second_total * second_factor
    joint_accum = first_accum * first_factor[..., None] + second_accum * second_factor[..., None]
    return (joint_max, joint_total, joint_accum)


def partial_softmax(scores, visible, value_heads, formula):
    scores = jnp.where(visible, scores, masked_score)
    highest = jnp.max(scores, axis=-1)
    weights = jnp.where(visible, jnp.exp(scores - highest[..., None]), 0.0)
    totals = jnp.sum(weights, axis=-1)
    accum = jnp.einsum(
        formula, weights.astype(jnp.bfloat16), value_heads, preferred_element_type=jnp.float32
    )
    return (highest, totals, accum)


def gathered_weights(
    queries,
    cache_keys,
    cache_values,
    new_keys,
    new_values,
    lengths,
    residual,
    norm_gain,
    w_gate,
    w_down,
):
    row_count, step_count, features = queries.shape
    positions = cache_keys.shape[1]
    per_group = features // (KVH * HD)
    inv_root = HD ** (-0.5)
    query_heads = queries.reshape(row_count, step_count, KVH, per_group, HD)
    key_heads = cache_keys.reshape(row_count, positions, KVH, HD)
    value_heads = cache_values.reshape(row_count, positions, KVH, HD)
    cached_scores = (
        jnp.einsum("rsjgd,rcjd->rsjgc", query_heads, key_heads, preferred_element_type=jnp.float32)
        * inv_root
    )
    offset = lax.axis_index("tp") * positions
    places = offset + lax.broadcasted_iota(jnp.int32, (row_count, positions), 1)
    visible = (places < lengths[:, None])[:, None, None, None, :]
    local_part = partial_softmax(cached_scores, visible, value_heads, "rsjgc,rcjd->rsjgd")
    merged = merged_2(local_part, "tp", combine_parts)
    fresh_key_heads = new_keys.reshape(row_count, step_count, KVH, HD)
    fresh_value_heads = new_values.reshape(row_count, step_count, KVH, HD)
    fresh_scores = (
        jnp.einsum(
            "rsjgd,rtjd->rsjgt", query_heads, fresh_key_heads, preferred_element_type=jnp.float32
        )
        * inv_root
    )
    causal = lax.broadcasted_iota(jnp.int32, (step_count, step_count), 0) >= lax.broadcasted_iota(
        jnp.int32, (step_count, step_count), 1
    )
    causal = causal[None, :, None, None, :]
    fresh_part = partial_softmax(fresh_scores, causal, fresh_value_heads, "rsjgt,rtjd->rsjgd")
    joint_max, joint_total, joint_accum = combine_parts(merged, fresh_part)
    context = (joint_accum / joint_total[..., None]).reshape(row_count, step_count, features)
    summed = residual.astype(jnp.float32) + context
    mean_square = jnp.mean(summed * summed, axis=-1, keepdims=True)
    normed = (summed * lax.rsqrt(mean_square + 1e-05) * norm_gain).astype(jnp.bfloat16)
    flat = normed.reshape(row_count * step_count, features)
    gate_policy, down_policy = (
        lax.all_gather(w_gate.astype(jnp.bfloat16), "grp", axis=0, tiled=True),
        lax.all_gather(w_down.astype(jnp.bfloat16), "grp", axis=0, tiled=True),
    )
    gate = jnp.dot(flat, gate_policy, preferred_element_type=jnp.float32)
    hidden = jax.nn.silu(gate).astype(jnp.bfloat16)
    partial_sum = lax.dot_general(
        hidden, down_policy, (((1,), (1,)), ((), ())), preferred_element_type=jnp.float32
    )
    mlp = lax.psum(partial_sum.astype(jnp.bfloat16), "tp").astype(jnp.float32)
    return (summed + mlp.reshape(row_count, step_count, features)).astype(jnp.bfloat16)


MESH = pl.DeviceIdType.MESH
BF16, F32 = jnp.bfloat16, jnp.float32


def layer_kernel(
    n_g,
    n_t,
    lengths_hbm,
    q_hbm,
    nk_hbm,
    nv_hbm,
    res_hbm,
    gain_hbm,
    ck_hbm,
    cv_hbm,
    wg_hbm,
    wd_hbm,
    out_ref,
    lengths_ref,
    q_in,
    nk_in,
    nv_in,
    res_in,
    gain,
    ck,
    cv,
    wg32,
    wd32,
    wg,
    wd,
    q_rows,
    res_rows,
    nk_rows,
    nv_rows,
    send_o,
    recv_o,
    send_x,
    recv_x,
    x_rows,
    x_flat,
    send_g,
    recv_g,
    send_h,
    recv_h,
    send_m,
    recv_m,
    send_f,
    load_sem,
    o_send_sem,
    o_recv_sem,
    m_send_sem,
    m_recv_sem,
    g_send_sem,
    g_recv_sem,
    h_send_sem,
    h_recv_sem,
    x_send_sem,
    x_recv_sem,
    f_send_sem,
    f_recv_sem,
):
    g, t = lax.axis_index("grp"), lax.axis_index("tp")
    rows, positions = ck.shape[0], ck.shape[1]
    steps = nk_in.shape[1]
    heads = gain.shape[0]
    units, depth = wg32.shape
    per_key = heads // KVH
    per_col = heads // n_g
    halves = per_key // per_col
    height = steps * per_col
    inv_root = HD ** (-0.5)
    group_rows = rows * steps
    half_t = n_t // 2

    peer_g = [g] + [lax.rem(g + k, n_g) for k in range(1, n_g)]
    peer_t = [t] + [lax.rem(t + k, n_t) for k in range(1, n_t)]
    far_first = sorted(range(n_t), key=lambda k: (k == 0, abs(k - half_t)))

    barrier = pltpu.get_barrier_semaphore()
    for peer in [(i, t) for i in peer_g[1:]] + [(g, k) for k in peer_t[1:]]:
        pl.semaphore_signal(barrier, inc=1, device_id=peer, device_id_type=MESH)

    loads = [
        pltpu.make_async_copy(source, target, load_sem.at[i])
        for i, (source, target) in enumerate(
            (
                (q_hbm, q_in),
                (lengths_hbm, lengths_ref),
                (ck_hbm, ck),
                (cv_hbm, cv),
                (nk_hbm, nk_in),
                (nv_hbm, nv_in),
                (res_hbm, res_in),
                (gain_hbm, gain),
                (wg_hbm, wg32),
                (wd_hbm, wd32),
            )
        )
    ]
    for load in loads:
        load.start()

    def blocks_of(at):
        first = (at % 2) * n_t + at // 2
        return first, first + half_t

    mine = (lax.rem(t, 2) * n_t + t // 2, lax.rem(t, 2) * n_t + t // 2 + half_t)

    def by_block(source, target):
        flat = jnp.concatenate([source[r].astype(F32) for r in range(rows)], axis=0)
        for h in range(heads):
            target[h // per_col, pl.ds(h % per_col, group_rows, stride=per_col), :] = flat[
                :, h * HD : (h + 1) * HD
            ]

    loads[0].wait()
    by_block(q_in, q_rows)
    loads[1].wait()
    loads[2].wait()
    lane_place = t * positions + lax.broadcasted_iota(jnp.int32, (halves * height, positions), 1)
    pieces, shown = [], []
    tall = halves * height
    blank = jnp.zeros((tall, HD), F32)
    for r in range(rows):
        visible = (lane_place < lengths_ref[r]).astype(F32)
        query = []
        for j in range(KVH):
            own = jnp.concatenate(
                [
                    q_rows[j * halves + i, r * height : (r + 1) * height]
                    for i in range(halves)
                ],
                axis=0,
            )
            query.append(jnp.concatenate([blank] * j + [own] + [blank] * (KVH - 1 - j), axis=1))
            shown.append(visible)
        pieces.append(
            lax.dot_general(
                jnp.concatenate(query, axis=0).astype(BF16),
                ck[r],
                (((1,), (1,)), ((), ())),
                preferred_element_type=F32,
            )
        )
    shown = jnp.concatenate(shown, axis=0) > 0.0
    scores = jnp.where(shown, jnp.concatenate(pieces, axis=0) * inv_root, masked_score)
    highest = jnp.max(scores, axis=-1, keepdims=True)
    weights = jnp.where(shown, jnp.exp(scores - highest), 0.0)
    total = jnp.sum(weights, axis=-1, keepdims=True)
    weights = weights.astype(BF16)
    loads[3].wait()
    accum = []
    for r in range(rows):
        wide = jnp.dot(
            weights[r * KVH * tall : (r + 1) * KVH * tall], cv[r], preferred_element_type=F32
        )
        for j in range(KVH):
            accum.append(wide[j * tall : (j + 1) * tall, j * HD : (j + 1) * HD])
    some = total > 0.0
    safe = jnp.where(some, total, 1.0)
    means = jnp.concatenate(accum, axis=0) / safe
    logs = jnp.where(some, highest + jnp.log(safe), masked_score)

    def of_owner(array, at, i):
        b = blocks_of(at)[i]
        starts = [
            (r * KVH + b // halves) * tall + (b % halves) * height for r in range(rows)
        ]
        return jnp.concatenate([array[at : at + height] for at in starts], axis=0)

    block_rows = rows * height
    off_lane = lax.broadcasted_iota(jnp.int32, (block_rows, HD), 1) - lax.broadcasted_iota(
        jnp.int32, (block_rows, HD), 0
    )
    diagonal = [off_lane == i * block_rows for i in range(2)]
    place = lax.broadcasted_iota(jnp.int32, (send_o.shape[1] - 2 * block_rows, HD), 0)

    log_rows = place.shape[0]
    spans = [(0, block_rows + log_rows), (block_rows + log_rows, block_rows)]

    def fill(at):
        lanes = sum(
            jnp.sum(jnp.where(diagonal[i], of_owner(logs, at, i), 0.0), axis=0, keepdims=True)
            for i in range(2)
        )
        high = lanes.astype(BF16).astype(F32)
        middle = (lanes - high).astype(BF16).astype(F32)
        low = lanes - high - middle
        terms = jnp.where(place == 0, high, jnp.where(place == 1, middle, low))
        send_o[at] = jnp.concatenate(
            [of_owner(means, at, 0), terms, of_owner(means, at, 1)], axis=0
        ).astype(BF16)

    def mean_copy(k, i):
        return pltpu.make_async_remote_copy(
            src_ref=send_o.at[peer_t[k], pl.ds(*spans[i])],
            dst_ref=recv_o.at[t, pl.ds(*spans[i])],
            send_sem=o_send_sem.at[i * n_t + k],
            recv_sem=o_recv_sem.at[i * n_t + k],
            device_id=(g, peer_t[k]),
            device_id_type=MESH,
        )

    def along_tp(k, i, source, target, send_sem, recv_sem):
        return pltpu.make_async_remote_copy(
            src_ref=source.at[i, peer_t[k]],
            dst_ref=target.at[i, t],
            send_sem=send_sem.at[i * n_t + k],
            recv_sem=recv_sem.at[i * n_t + k],
            device_id=(g, peer_t[k]),
            device_id_type=MESH,
        )

    for at in range(n_t):
        fill(at)
    pl.semaphore_wait(barrier, n_g + n_t - 2)
    row_copies = [[mean_copy(k, i) for k in far_first[:-1]] for i in range(2)]
    for copy in row_copies[0] + row_copies[1]:
        copy.start()
    recv_o[t] = send_o[t]

    for load in loads[4:8]:
        load.wait()
    by_block(res_in, res_rows)
    for source, target in ((nk_in, nk_rows), (nv_in, nv_rows)):
        flat = jnp.concatenate([source[r].astype(F32) for r in range(rows)], axis=0)
        for j in range(KVH):
            target[j] = flat[:, j * HD : (j + 1) * HD]

    def new_tokens(tokens, at, b):
        held = tokens[b // halves]
        return jnp.concatenate(
            [
                jnp.broadcast_to(held[r * steps + at : r * steps + at + 1], (height, HD))
                for r in range(rows)
            ],
            axis=0,
        )

    step_of = lax.broadcasted_iota(jnp.int32, (block_rows, 1), 0) & (height - 1)
    seen = [step_of >= at * per_col for at in range(steps)]
    fresh = [
        [
            jnp.where(
                seen[at],
                jnp.sum(q_rows[b] * new_tokens(nk_rows, at, b), axis=-1, keepdims=True)
                * inv_root,
                masked_score,
            )
            for at in range(steps)
        ]
        for b in mine
    ]
    new_held = [[new_tokens(nv_rows, at, b) for at in range(steps)] for b in mine]
    loads[8].wait()
    spare = jnp.zeros((wg.shape[0] - units, depth), F32)
    wg[...] = jnp.concatenate([wg32[...], spare], axis=0).astype(BF16)

    def finish_context(i):
        logs = []
        for at in range(n_t):
            terms = recv_o[at, block_rows : block_rows + log_rows].astype(F32)
            lanes = terms[0:1] + terms[1:2] + terms[2:3]
            logs.append(jnp.sum(jnp.where(diagonal[i], lanes, 0.0), axis=-1, keepdims=True))
        joint = functools.reduce(jnp.maximum, logs + fresh[i])
        total, accum = 0.0, 0.0
        for at in range(n_t):
            weight = jnp.exp(logs[at] - joint)
            total = total + weight
            held = recv_o[at, i * spans[1][0] : i * spans[1][0] + block_rows]
            accum = accum + weight * held.astype(F32)
        for at in range(steps):
            weight = jnp.where(seen[at], jnp.exp(fresh[i][at] - joint), 0.0)
            total = total + weight
            accum = accum + weight.astype(BF16).astype(F32) * new_held[i][at]
        send_x[i] = (res_rows[mine[i]] + accum / total).astype(BF16)

    class Spread:
        def __init__(self, source, target, send_sem, recv_sem):
            self.refs = source, target, send_sem, recv_sem

        def each(self, action, parts):
            source, target, send_sem, recv_sem = self.refs
            for i in parts:
                for k in far_first:
                    copy = pltpu.make_async_remote_copy(
                        src_ref=source.at[i],
                        dst_ref=target(g),
                        send_sem=send_sem.at[i * n_t + k],
                        recv_sem=recv_sem.at[g],
                        device_id=(mine[i], peer_t[k]),
                        device_id_type=MESH,
                    )
                    if k:
                        action(copy)
                    else:
                        pl.when(mine[i] != g)(functools.partial(action, copy))

        def start(self, i):
            self.each(lambda copy: copy.start(), (i,))
            source, target, _, recv_sem = self.refs
            here = pltpu.make_async_copy(source.at[i], target(g), recv_sem.at[g])
            pl.when(mine[i] == g)(here.start)

        def wait_send(self):
            self.each(lambda copy: copy.wait_send(), range(2))

        def wait_recv(self, parts):
            source, target, _, recv_sem = self.refs
            for i in parts:
                pltpu.make_async_copy(source.at[0], target(i), recv_sem.at[i]).wait()

    x_spread = Spread(send_x, lambda i: recv_x.at[i], x_send_sem, x_recv_sem)
    for i in range(2):
        for copy in row_copies[i]:
            copy.wait_recv()
        finish_context(i)
        x_spread.start(i)

    parts = [[blocks_of(at)[i] for at in range(n_t)] for i in range(2)]
    part_rows = n_t * group_rows
    gains = [gain[pl.ds(g * per_col + c, 1)] for c in range(per_col)]

    def part_gate(i):
        x_spread.wait_recv(parts[i])
        x_rows[i] = jnp.concatenate([recv_x[b].astype(F32) for b in parts[i]], axis=0)
        columns = [
            x_rows.at[i][pl.ds(c, part_rows, stride=per_col), :] for c in range(per_col)
        ]
        squares = jnp.sum(
            functools.reduce(jnp.add, [c * c for c in columns]), axis=-1, keepdims=True
        )
        scaled = jnp.concatenate([c * by for c, by in zip(columns, gains)], axis=1).astype(BF16)
        gate = lax.dot_general(
            scaled, wg[...], (((1,), (1,)), ((), ())), preferred_element_type=F32
        )
        spare_lane = lax.broadcasted_iota(jnp.int32, gate.shape, 1) >= units
        gate = jnp.where(spare_lane, squares, gate)
        for at, b in enumerate(parts[i]):
            send_g[b] = gate[at * group_rows : (at + 1) * group_rows].astype(BF16)
        return columns

    def along_grp(k, source, target, send_sem, recv_sem):
        return pltpu.make_async_remote_copy(
            src_ref=source,
            dst_ref=target.at[g],
            send_sem=send_sem.at[k - 1],
            recv_sem=recv_sem.at[k - 1],
            device_id=(peer_g[k], t),
            device_id_type=MESH,
        )

    gate_copies = [
        along_grp(k, send_g.at[peer_g[k]], recv_g, g_send_sem, g_recv_sem) for k in range(1, n_g)
    ]
    held_columns = []
    for i in range(2):
        held_columns.append(part_gate(i))
        for k in range(1, n_g):
            in_part = functools.reduce(jnp.logical_or, [peer_g[k] == b for b in parts[i]])
            pl.when(in_part)(gate_copies[k - 1].start)
    for i in range(2):
        wide = jnp.concatenate(held_columns[i], axis=1)
        for at, b in enumerate(parts[i]):
            x_flat[b] = wide[at * group_rows : (at + 1) * group_rows]
    recv_g[g] = send_g[g]
    loads[9].wait()
    wd[...] = jnp.concatenate([wd32[...], spare], axis=0).astype(BF16)
    for copy in gate_copies:
        copy.wait_recv()
    whole = functools.reduce(jnp.add, [recv_g[i].astype(F32) for i in range(n_g)])
    square = whole[:, units : units + 1]
    whole = whole * lax.rsqrt(square / (heads * HD) + 1e-05)
    own_hidden = (whole / (1.0 + jnp.exp(-whole))).astype(BF16)

    send_h[...] = own_hidden
    hidden_copies = [
        pltpu.make_async_remote_copy(
            src_ref=send_h,
            dst_ref=recv_h.at[g],
            send_sem=h_send_sem.at[k],
            recv_sem=h_recv_sem.at[g],
            device_id=(peer_g[k], t),
            device_id_type=MESH,
        )
        for k in range(1, n_g)
    ]
    for copy in hidden_copies:
        copy.start()
    pltpu.make_async_copy(send_h, recv_h.at[g], h_recv_sem.at[g]).start()

    mlp_copies = [
        [along_tp(k, i, send_m, recv_m, m_send_sem, m_recv_sem) for k in far_first[:-1]]
        for i in range(2)
    ]
    for i in range(2):
        for b in parts[i]:
            pltpu.make_async_copy(send_h, recv_h.at[b], h_recv_sem.at[b]).wait()
        hidden = jnp.concatenate([recv_h[b].astype(F32) for b in parts[i]], axis=0).astype(BF16)
        mlp = jnp.dot(hidden, wd[...], preferred_element_type=F32)
        for at in range(n_t):
            send_m[i, at] = mlp[at * group_rows : (at + 1) * group_rows].astype(BF16)
        for copy in mlp_copies[i]:
            copy.start()
        recv_m[i, t] = send_m[i, t]

    def out_columns(i):
        return out_ref.at[:, :, pl.ds(pl.multiple_of(i * depth, depth), depth)]

    f_spread = Spread(send_f, out_columns, f_send_sem, f_recv_sem)
    for i in range(2):
        for copy in mlp_copies[i]:
            copy.wait_recv()
        done = functools.reduce(jnp.add, [recv_m[i, at].astype(F32) for at in range(n_t)])
        done = (x_flat[mine[i]] + done).astype(BF16)
        for r in range(rows):
            send_f[i, r] = done[r * steps : (r + 1) * steps]
        f_spread.start(i)
    for copy in row_copies[0] + row_copies[1] + gate_copies + hidden_copies:
        copy.wait_send()
    for copy in mlp_copies[0] + mlp_copies[1]:
        copy.wait_send()
    x_spread.wait_send()
    f_spread.wait_recv(range(n_g))
    f_spread.wait_send()


def moved_activations(
    n_g,
    n_t,
    queries,
    cache_keys,
    cache_values,
    new_keys,
    new_values,
    lengths,
    residual,
    norm_gain,
    w_gate,
    w_down,
):
    rows, steps, features = queries.shape
    positions, kv_width = cache_keys.shape[1:]
    depth, units = w_gate.shape
    heads = features // HD
    per_col = heads // n_g
    height = steps * per_col
    group_rows = rows * steps
    wide = (units // HD + 1) * HD
    hbm = pl.BlockSpec(memory_space=pltpu.HBM)
    dma = pltpu.SemaphoreType.DMA
    return pl.pallas_call(
        functools.partial(layer_kernel, n_g, n_t),
        out_shape=pltpu.VMEM(queries.shape, BF16),
        in_specs=[hbm] * 10,
        out_specs=pl.BlockSpec(memory_space=pltpu.VMEM),
        scratch_shapes=[
            pltpu.SMEM(lengths.shape, jnp.int32),
            pltpu.VMEM(queries.shape, BF16),
            pltpu.VMEM(new_keys.shape, BF16),
            pltpu.VMEM(new_values.shape, BF16),
            pltpu.VMEM(residual.shape, BF16),
            pltpu.VMEM((heads, HD), F32),
            pltpu.VMEM(cache_keys.shape, BF16),
            pltpu.VMEM(cache_values.shape, BF16),
            pltpu.VMEM((units, depth), F32),
            pltpu.VMEM((units, depth), F32),
            pltpu.VMEM((wide, depth), BF16),
            pltpu.VMEM((wide, depth), BF16),
            pltpu.VMEM((n_g, rows * height, HD), F32),
            pltpu.VMEM((n_g, rows * height, HD), F32),
            pltpu.VMEM((KVH, group_rows, HD), F32),
            pltpu.VMEM((KVH, group_rows, HD), F32),
            pltpu.VMEM((n_t, 2 * rows * height + 16, HD), BF16),
            pltpu.VMEM((n_t, 2 * rows * height + 16, HD), BF16),
            pltpu.VMEM((2, rows * height, HD), BF16),
            pltpu.VMEM((n_g, rows * height, HD), BF16),
            pltpu.VMEM((2, n_t * rows * height, HD), F32),
            pltpu.VMEM((n_g, group_rows, depth), F32),
            pltpu.VMEM((n_g, group_rows, wide), BF16),
            pltpu.VMEM((n_g, group_rows, wide), BF16),
            pltpu.VMEM((group_rows, wide), BF16),
            pltpu.VMEM((n_g, group_rows, wide), BF16),
            pltpu.VMEM((2, n_t, group_rows, depth), BF16),
            pltpu.VMEM((2, n_t, group_rows, depth), BF16),
            pltpu.VMEM((2, rows, steps, depth), BF16),
            dma((10,)),
        ]
        + [dma((2 * n_t,))] * 4
        + [dma((n_g,))] * 8,
        compiler_params=pltpu.CompilerParams(
            collective_id=0, has_side_effects=True, vmem_limit_bytes=40 * 1024 * 1024
        ),
    )(
        *(
            pltpu.with_memory_space_constraint(array, pltpu.HBM)
            for array in (
                lengths,
                queries,
                new_keys,
                new_values,
                residual,
                norm_gain.reshape(heads, HD),
                cache_keys,
                cache_values,
                w_gate.T,
                w_down.T,
            )
        ),
    )


def shards(n_g, n_t, *arrays):
    queries, cache_keys = arrays[0], arrays[1]
    rows, steps, features = queries.shape
    heads = features // HD
    kv_heads = cache_keys.shape[2] // HD
    even = (
        n_g == 2 * n_t
        and n_t % 2 == 0
        and heads % n_g == 0
        and n_g % kv_heads == 0
        and steps * (heads // n_g) == 8
        and rows % 2 == 0
        and rows * steps == 8
    )
    if even:
        return moved_activations(n_g, n_t, *arrays)
    return gathered_weights(*arrays)


def solution(mesh):
    return jax.shard_map(
        functools.partial(shards, mesh.shape["grp"], mesh.shape["tp"]),
        mesh=mesh,
        in_specs=(
            P("grp", None, None),
            P("grp", "tp", None),
            P("grp", "tp", None),
            P("grp", None, None),
            P("grp", None, None),
            P("grp"),
            P("grp", None, None),
            P(),
            P("grp", "tp"),
            P("grp", "tp"),
        ),
        out_specs=P("grp", None, None),
        check_vma=False,
    )
```

```python
import functools

import jax
import jax.numpy as jnp
from jax import lax
from jax.experimental import pallas as pl
from jax.experimental.pallas import tpu as pltpu
from jax.sharding import PartitionSpec as P

HD = 128
KVH = 4


masked_score = -1e30


def merged_2(shard, axis, join):
    gathered = jax.tree.map(
        lambda a, kind: lax.all_gather(a.astype(kind), axis),
        shard,
        jax.tree.map(lambda a: jnp.bfloat16 if a.dtype == jnp.float32 else a.dtype, shard),
    )

    def take(source):
        return jax.tree.map(
            lambda a, own: lax.dynamic_index_in_dim(a, source, 0, False).astype(own.dtype),
            gathered,
            shard,
        )

    return lax.fori_loop(
        1, lax.axis_size(axis), lambda source, state: join(state, take(source)), take(0)
    )


def combine_parts(earlier, later):
    first_max, first_total, first_accum = earlier
    second_max, second_total, second_accum = later
    joint_max = jnp.maximum(first_max, second_max)
    first_factor = jnp.exp(first_max - joint_max)
    second_factor = jnp.exp(second_max - joint_max)
    joint_total = first_total * first_factor + second_total * second_factor
    joint_accum = first_accum * first_factor[..., None] + second_accum * second_factor[..., None]
    return (joint_max, joint_total, joint_accum)


def partial_softmax(scores, visible, value_heads, formula):
    scores = jnp.where(visible, scores, masked_score)
    highest = jnp.max(scores, axis=-1)
    weights = jnp.where(visible, jnp.exp(scores - highest[..., None]), 0.0)
    totals = jnp.sum(weights, axis=-1)
    accum = jnp.einsum(
        formula, weights.astype(jnp.bfloat16), value_heads, preferred_element_type=jnp.float32
    )
    return (highest, totals, accum)


def gathered_weights(
    queries,
    cache_keys,
    cache_values,
    new_keys,
    new_values,
    lengths,
    residual,
    norm_gain,
    w_gate,
    w_down,
):
    row_count, step_count, features = queries.shape
    positions = cache_keys.shape[1]
    per_group = features // (KVH * HD)
    inv_root = HD ** (-0.5)
    query_heads = queries.reshape(row_count, step_count, KVH, per_group, HD)
    key_heads = cache_keys.reshape(row_count, positions, KVH, HD)
    value_heads = cache_values.reshape(row_count, positions, KVH, HD)
    cached_scores = (
        jnp.einsum("rsjgd,rcjd->rsjgc", query_heads, key_heads, preferred_element_type=jnp.float32)
        * inv_root
    )
    offset = lax.axis_index("tp") * positions
    places = offset + lax.broadcasted_iota(jnp.int32, (row_count, positions), 1)
    visible = (places < lengths[:, None])[:, None, None, None, :]
    local_part = partial_softmax(cached_scores, visible, value_heads, "rsjgc,rcjd->rsjgd")
    merged = merged_2(local_part, "tp", combine_parts)
    fresh_key_heads = new_keys.reshape(row_count, step_count, KVH, HD)
    fresh_value_heads = new_values.reshape(row_count, step_count, KVH, HD)
    fresh_scores = (
        jnp.einsum(
            "rsjgd,rtjd->rsjgt", query_heads, fresh_key_heads, preferred_element_type=jnp.float32
        )
        * inv_root
    )
    causal = lax.broadcasted_iota(jnp.int32, (step_count, step_count), 0) >= lax.broadcasted_iota(
        jnp.int32, (step_count, step_count), 1
    )
    causal = causal[None, :, None, None, :]
    fresh_part = partial_softmax(fresh_scores, causal, fresh_value_heads, "rsjgt,rtjd->rsjgd")
    joint_max, joint_total, joint_accum = combine_parts(merged, fresh_part)
    context = (joint_accum / joint_total[..., None]).reshape(row_count, step_count, features)
    summed = residual.astype(jnp.float32) + context
    mean_square = jnp.mean(summed * summed, axis=-1, keepdims=True)
    normed = (summed * lax.rsqrt(mean_square + 1e-05) * norm_gain).astype(jnp.bfloat16)
    flat = normed.reshape(row_count * step_count, features)
    gate_policy, down_policy = (
        lax.all_gather(w_gate.astype(jnp.bfloat16), "grp", axis=0, tiled=True),
        lax.all_gather(w_down.astype(jnp.bfloat16), "grp", axis=0, tiled=True),
    )
    gate = jnp.dot(flat, gate_policy, preferred_element_type=jnp.float32)
    hidden = jax.nn.silu(gate).astype(jnp.bfloat16)
    partial_sum = lax.dot_general(
        hidden, down_policy, (((1,), (1,)), ((), ())), preferred_element_type=jnp.float32
    )
    mlp = lax.psum(partial_sum.astype(jnp.bfloat16), "tp").astype(jnp.float32)
    return (summed + mlp.reshape(row_count, step_count, features)).astype(jnp.bfloat16)


MESH = pl.DeviceIdType.MESH
BF16, F32 = jnp.bfloat16, jnp.float32


def layer_kernel(
    n_g,
    n_t,
    lengths_hbm,
    q_hbm,
    nk_hbm,
    nv_hbm,
    res_hbm,
    gain_hbm,
    ck_hbm,
    cv_hbm,
    wg_hbm,
    wd_hbm,
    out_ref,
    lengths_ref,
    q_in,
    nk_in,
    nv_in,
    res_in,
    gain,
    ck,
    cv,
    wg32,
    wd32,
    wg,
    wd,
    q_rows,
    res_rows,
    nk_rows,
    nv_rows,
    send_o,
    recv_o,
    send_x,
    recv_x,
    x_rows,
    x_flat,
    send_g,
    recv_g,
    send_h,
    recv_h,
    send_m,
    recv_m,
    send_f,
    load_sem,
    o_send_sem,
    o_recv_sem,
    m_send_sem,
    m_recv_sem,
    g_send_sem,
    g_recv_sem,
    h_send_sem,
    h_recv_sem,
    x_send_sem,
    x_recv_sem,
    f_send_sem,
    f_recv_sem,
):
    g, t = lax.axis_index("grp"), lax.axis_index("tp")
    rows, positions = ck.shape[0], ck.shape[1]
    steps = nk_in.shape[1]
    heads = gain.shape[0]
    units, depth = wg32.shape
    per_key = heads // KVH
    per_col = heads // n_g
    halves = per_key // per_col
    height = steps * per_col
    inv_root = HD ** (-0.5)
    group_rows = rows * steps
    half_t = n_t // 2

    peer_g = [g] + [lax.rem(g + k, n_g) for k in range(1, n_g)]
    peer_t = [t] + [lax.rem(t + k, n_t) for k in range(1, n_t)]
    far_first = sorted(range(n_t), key=lambda k: (k == 0, abs(k - half_t)))

    barrier = pltpu.get_barrier_semaphore()
    for peer in [(i, t) for i in peer_g[1:]] + [(g, k) for k in peer_t[1:]]:
        pl.semaphore_signal(barrier, inc=1, device_id=peer, device_id_type=MESH)

    loads = [
        pltpu.make_async_copy(source, target, load_sem.at[i])
        for i, (source, target) in enumerate(
            (
                (q_hbm, q_in),
                (lengths_hbm, lengths_ref),
                (ck_hbm, ck),
                (cv_hbm, cv),
                (nk_hbm, nk_in),
                (nv_hbm, nv_in),
                (res_hbm, res_in),
                (gain_hbm, gain),
                (wg_hbm, wg32),
                (wd_hbm, wd32),
            )
        )
    ]
    for load in loads:
        load.start()

    def blocks_of(at):
        first = (at % 2) * n_t + at // 2
        return first, first + half_t

    mine = (lax.rem(t, 2) * n_t + t // 2, lax.rem(t, 2) * n_t + t // 2 + half_t)

    def by_block(source, target):
        flat = jnp.concatenate([source[r].astype(F32) for r in range(rows)], axis=0)
        for h in range(heads):
            target[h // per_col, pl.ds(h % per_col, group_rows, stride=per_col), :] = flat[
                :, h * HD : (h + 1) * HD
            ]

    loads[0].wait()
    by_block(q_in, q_rows)
    loads[1].wait()
    loads[2].wait()
    lane_place = t * positions + lax.broadcasted_iota(jnp.int32, (halves * height, positions), 1)
    pieces, shown = [], []
    tall = halves * height
    blank = jnp.zeros((tall, HD), F32)
    for r in range(rows):
        visible = (lane_place < lengths_ref[r]).astype(F32)
        query = []
        for j in range(KVH):
            own = jnp.concatenate(
                [
                    q_rows[j * halves + i, r * height : (r + 1) * height]
                    for i in range(halves)
                ],
                axis=0,
            )
            query.append(jnp.concatenate([blank] * j + [own] + [blank] * (KVH - 1 - j), axis=1))
            shown.append(visible)
        pieces.append(
            lax.dot_general(
                jnp.concatenate(query, axis=0).astype(BF16),
                ck[r],
                (((1,), (1,)), ((), ())),
                preferred_element_type=F32,
            )
        )
    shown = jnp.concatenate(shown, axis=0) > 0.0
    scores = jnp.where(shown, jnp.concatenate(pieces, axis=0) * inv_root, masked_score)
    highest = jnp.max(scores, axis=-1, keepdims=True)
    weights = jnp.where(shown, jnp.exp(scores - highest), 0.0)
    total = jnp.sum(weights, axis=-1, keepdims=True)
    weights = weights.astype(BF16)
    loads[3].wait()
    accum = []
    for r in range(rows):
        wide = jnp.dot(
            weights[r * KVH * tall : (r + 1) * KVH * tall], cv[r], preferred_element_type=F32
        )
        for j in range(KVH):
            accum.append(wide[j * tall : (j + 1) * tall, j * HD : (j + 1) * HD])
    some = total > 0.0
    safe = jnp.where(some, total, 1.0)
    means = jnp.concatenate(accum, axis=0) / safe
    logs = jnp.where(some, highest + jnp.log(safe), masked_score)

    def of_owner(array, at, i):
        b = blocks_of(at)[i]
        starts = [
            (r * KVH + b // halves) * tall + (b % halves) * height for r in range(rows)
        ]
        return jnp.concatenate([array[at : at + height] for at in starts], axis=0)

    block_rows = rows * height
    off_lane = lax.broadcasted_iota(jnp.int32, (block_rows, HD), 1) - lax.broadcasted_iota(
        jnp.int32, (block_rows, HD), 0
    )
    diagonal = [off_lane == i * block_rows for i in range(2)]
    place = lax.broadcasted_iota(jnp.int32, (send_o.shape[1] - 2 * block_rows, HD), 0)

    log_rows = place.shape[0]
    spans = [(0, block_rows + log_rows), (block_rows + log_rows, block_rows)]

    def fill(at):
        lanes = sum(
            jnp.sum(jnp.where(diagonal[i], of_owner(logs, at, i), 0.0), axis=0, keepdims=True)
            for i in range(2)
        )
        high = lanes.astype(BF16).astype(F32)
        middle = (lanes - high).astype(BF16).astype(F32)
        low = lanes - high - middle
        terms = jnp.where(place == 0, high, jnp.where(place == 1, middle, low))
        send_o[at] = jnp.concatenate(
            [of_owner(means, at, 0), terms, of_owner(means, at, 1)], axis=0
        ).astype(BF16)

    def mean_copy(k, i):
        return pltpu.make_async_remote_copy(
            src_ref=send_o.at[peer_t[k], pl.ds(*spans[i])],
            dst_ref=recv_o.at[t, pl.ds(*spans[i])],
            send_sem=o_send_sem.at[i * n_t + k],
            recv_sem=o_recv_sem.at[i * n_t + k],
            device_id=(g, peer_t[k]),
            device_id_type=MESH,
        )

    def along_tp(k, i, source, target, send_sem, recv_sem):
        return pltpu.make_async_remote_copy(
            src_ref=source.at[i, peer_t[k]],
            dst_ref=target.at[i, t],
            send_sem=send_sem.at[i * n_t + k],
            recv_sem=recv_sem.at[i * n_t + k],
            device_id=(g, peer_t[k]),
            device_id_type=MESH,
        )

    for at in range(n_t):
        fill(at)
    pl.semaphore_wait(barrier, n_g + n_t - 2)
    row_copies = [[mean_copy(k, i) for k in far_first[:-1]] for i in range(2)]
    for copy in row_copies[0] + row_copies[1]:
        copy.start()
    recv_o[t] = send_o[t]

    for load in loads[4:8]:
        load.wait()
    by_block(res_in, res_rows)
    for source, target in ((nk_in, nk_rows), (nv_in, nv_rows)):
        flat = jnp.concatenate([source[r].astype(F32) for r in range(rows)], axis=0)
        for j in range(KVH):
            target[j] = flat[:, j * HD : (j + 1) * HD]

    def new_tokens(tokens, at, b):
        held = tokens[b // halves]
        return jnp.concatenate(
            [
                jnp.broadcast_to(held[r * steps + at : r * steps + at + 1], (height, HD))
                for r in range(rows)
            ],
            axis=0,
        )

    step_of = lax.broadcasted_iota(jnp.int32, (block_rows, 1), 0) & (height - 1)
    seen = [step_of >= at * per_col for at in range(steps)]
    fresh = [
        [
            jnp.where(
                seen[at],
                jnp.sum(q_rows[b] * new_tokens(nk_rows, at, b), axis=-1, keepdims=True)
                * inv_root,
                masked_score,
            )
            for at in range(steps)
        ]
        for b in mine
    ]
    new_held = [[new_tokens(nv_rows, at, b) for at in range(steps)] for b in mine]
    loads[8].wait()
    spare = jnp.zeros((wg.shape[0] - units, depth), F32)
    wg[...] = jnp.concatenate([wg32[...], spare], axis=0).astype(BF16)

    def finish_context(i):
        logs = []
        for at in range(n_t):
            terms = recv_o[at, block_rows : block_rows + log_rows].astype(F32)
            lanes = terms[0:1] + terms[1:2] + terms[2:3]
            logs.append(jnp.sum(jnp.where(diagonal[i], lanes, 0.0), axis=-1, keepdims=True))
        joint = functools.reduce(jnp.maximum, logs + fresh[i])
        total, accum = 0.0, 0.0
        for at in range(n_t):
            weight = jnp.exp(logs[at] - joint)
            total = total + weight
            held = recv_o[at, i * spans[1][0] : i * spans[1][0] + block_rows]
            accum = accum + weight * held.astype(F32)
        for at in range(steps):
            weight = jnp.where(seen[at], jnp.exp(fresh[i][at] - joint), 0.0)
            total = total + weight
            accum = accum + weight.astype(BF16).astype(F32) * new_held[i][at]
        send_x[i] = (res_rows[mine[i]] + accum / total).astype(BF16)

    class Spread:
        def __init__(self, source, target, send_sem, recv_sem):
            self.refs = source, target, send_sem, recv_sem

        def each(self, action, parts):
            source, target, send_sem, recv_sem = self.refs
            for i in parts:
                for k in far_first:
                    copy = pltpu.make_async_remote_copy(
                        src_ref=source.at[i],
                        dst_ref=target(g),
                        send_sem=send_sem.at[i * n_t + k],
                        recv_sem=recv_sem.at[g],
                        device_id=(mine[i], peer_t[k]),
                        device_id_type=MESH,
                    )
                    if k:
                        action(copy)
                    else:
                        pl.when(mine[i] != g)(functools.partial(action, copy))

        def start(self, i):
            self.each(lambda copy: copy.start(), (i,))
            source, target, _, recv_sem = self.refs
            here = pltpu.make_async_copy(source.at[i], target(g), recv_sem.at[g])
            pl.when(mine[i] == g)(here.start)

        def wait_send(self):
            self.each(lambda copy: copy.wait_send(), range(2))

        def wait_recv(self, parts):
            source, target, _, recv_sem = self.refs
            for i in parts:
                pltpu.make_async_copy(source.at[0], target(i), recv_sem.at[i]).wait()

    x_spread = Spread(send_x, lambda i: recv_x.at[i], x_send_sem, x_recv_sem)
    for i in range(2):
        for copy in row_copies[i]:
            copy.wait_recv()
        finish_context(i)
        x_spread.start(i)

    parts = [[blocks_of(at)[i] for at in range(n_t)] for i in range(2)]
    all_rows = n_g * group_rows
    gains = [gain[pl.ds(g * per_col + c, 1)] for c in range(per_col)]

    def part_gate():
        x_spread.wait_recv(range(n_g))
        x_rows[...] = recv_x[...].astype(F32).reshape(x_rows.shape)
        columns = [x_rows[pl.ds(c, all_rows, stride=per_col), :] for c in range(per_col)]
        squares = jnp.sum(
            functools.reduce(jnp.add, [c * c for c in columns]), axis=-1, keepdims=True
        )
        scaled = jnp.concatenate([c * by for c, by in zip(columns, gains)], axis=1).astype(BF16)
        gate = lax.dot_general(
            scaled, wg[...], (((1,), (1,)), ((), ())), preferred_element_type=F32
        )
        spare_lane = lax.broadcasted_iota(jnp.int32, gate.shape, 1) >= units
        gate = jnp.where(spare_lane, squares, gate)
        for b in range(n_g):
            send_g[b] = gate[b * group_rows : (b + 1) * group_rows].astype(BF16)
        return columns

    def along_grp(k, source, target, send_sem, recv_sem):
        return pltpu.make_async_remote_copy(
            src_ref=source,
            dst_ref=target.at[g],
            send_sem=send_sem.at[k - 1],
            recv_sem=recv_sem.at[k - 1],
            device_id=(peer_g[k], t),
            device_id_type=MESH,
        )

    gate_copies = [
        along_grp(k, send_g.at[peer_g[k]], recv_g, g_send_sem, g_recv_sem) for k in range(1, n_g)
    ]
    columns = part_gate()
    for copy in gate_copies:
        copy.start()
    x_flat[...] = jnp.concatenate(columns, axis=1).reshape(x_flat.shape)
    recv_g[g] = send_g[g]
    loads[9].wait()
    wd[...] = jnp.concatenate([wd32[...], spare], axis=0).astype(BF16)
    for copy in gate_copies:
        copy.wait_recv()
    whole = functools.reduce(jnp.add, [recv_g[i].astype(F32) for i in range(n_g)])
    square = whole[:, units : units + 1]
    whole = whole * lax.rsqrt(square / (heads * HD) + 1e-05)
    own_hidden = (whole / (1.0 + jnp.exp(-whole))).astype(BF16)

    send_h[...] = own_hidden
    hidden_copies = [
        pltpu.make_async_remote_copy(
            src_ref=send_h,
            dst_ref=recv_h.at[g],
            send_sem=h_send_sem.at[k],
            recv_sem=h_recv_sem.at[g],
            device_id=(peer_g[k], t),
            device_id_type=MESH,
        )
        for k in range(1, n_g)
    ]
    for copy in hidden_copies:
        copy.start()
    pltpu.make_async_copy(send_h, recv_h.at[g], h_recv_sem.at[g]).start()

    mlp_copies = [
        [along_tp(k, i, send_m, recv_m, m_send_sem, m_recv_sem) for k in far_first[:-1]]
        for i in range(2)
    ]
    for i in range(2):
        for b in parts[i]:
            pltpu.make_async_copy(send_h, recv_h.at[b], h_recv_sem.at[b]).wait()
        hidden = jnp.concatenate([recv_h[b].astype(F32) for b in parts[i]], axis=0).astype(BF16)
        mlp = jnp.dot(hidden, wd[...], preferred_element_type=F32)
        for at in range(n_t):
            send_m[i, at] = mlp[at * group_rows : (at + 1) * group_rows].astype(BF16)
        for copy in mlp_copies[i]:
            copy.start()
        recv_m[i, t] = send_m[i, t]

    def out_columns(i):
        return out_ref.at[:, :, pl.ds(pl.multiple_of(i * depth, depth), depth)]

    f_spread = Spread(send_f, out_columns, f_send_sem, f_recv_sem)
    for i in range(2):
        for copy in mlp_copies[i]:
            copy.wait_recv()
        done = functools.reduce(jnp.add, [recv_m[i, at].astype(F32) for at in range(n_t)])
        done = (x_flat[mine[i]] + done).astype(BF16)
        for r in range(rows):
            send_f[i, r] = done[r * steps : (r + 1) * steps]
        f_spread.start(i)
    for copy in row_copies[0] + row_copies[1] + gate_copies + hidden_copies:
        copy.wait_send()
    for copy in mlp_copies[0] + mlp_copies[1]:
        copy.wait_send()
    x_spread.wait_send()
    f_spread.wait_recv(range(n_g))
    f_spread.wait_send()


def moved_activations(
    n_g,
    n_t,
    queries,
    cache_keys,
    cache_values,
    new_keys,
    new_values,
    lengths,
    residual,
    norm_gain,
    w_gate,
    w_down,
):
    rows, steps, features = queries.shape
    positions, kv_width = cache_keys.shape[1:]
    depth, units = w_gate.shape
    heads = features // HD
    per_col = heads // n_g
    height = steps * per_col
    group_rows = rows * steps
    wide = (units // HD + 1) * HD
    hbm = pl.BlockSpec(memory_space=pltpu.HBM)
    dma = pltpu.SemaphoreType.DMA
    return pl.pallas_call(
        functools.partial(layer_kernel, n_g, n_t),
        out_shape=pltpu.VMEM(queries.shape, BF16),
        in_specs=[hbm] * 10,
        out_specs=pl.BlockSpec(memory_space=pltpu.VMEM),
        scratch_shapes=[
            pltpu.SMEM(lengths.shape, jnp.int32),
            pltpu.VMEM(queries.shape, BF16),
            pltpu.VMEM(new_keys.shape, BF16),
            pltpu.VMEM(new_values.shape, BF16),
            pltpu.VMEM(residual.shape, BF16),
            pltpu.VMEM((heads, HD), F32),
            pltpu.VMEM(cache_keys.shape, BF16),
            pltpu.VMEM(cache_values.shape, BF16),
            pltpu.VMEM((units, depth), F32),
            pltpu.VMEM((units, depth), F32),
            pltpu.VMEM((wide, depth), BF16),
            pltpu.VMEM((wide, depth), BF16),
            pltpu.VMEM((n_g, rows * height, HD), F32),
            pltpu.VMEM((n_g, rows * height, HD), F32),
            pltpu.VMEM((KVH, group_rows, HD), F32),
            pltpu.VMEM((KVH, group_rows, HD), F32),
            pltpu.VMEM((n_t, 2 * rows * height + 16, HD), BF16),
            pltpu.VMEM((n_t, 2 * rows * height + 16, HD), BF16),
            pltpu.VMEM((2, rows * height, HD), BF16),
            pltpu.VMEM((n_g, rows * height, HD), BF16),
            pltpu.VMEM((n_g * rows * height, HD), F32),
            pltpu.VMEM((n_g, group_rows, depth), F32),
            pltpu.VMEM((n_g, group_rows, wide), BF16),
            pltpu.VMEM((n_g, group_rows, wide), BF16),
            pltpu.VMEM((group_rows, wide), BF16),
            pltpu.VMEM((n_g, group_rows, wide), BF16),
            pltpu.VMEM((2, n_t, group_rows, depth), BF16),
            pltpu.VMEM((2, n_t, group_rows, depth), BF16),
            pltpu.VMEM((2, rows, steps, depth), BF16),
            dma((10,)),
        ]
        + [dma((2 * n_t,))] * 4
        + [dma((n_g,))] * 8,
        compiler_params=pltpu.CompilerParams(
            collective_id=0, has_side_effects=True, vmem_limit_bytes=40 * 1024 * 1024
        ),
    )(
        *(
            pltpu.with_memory_space_constraint(array, pltpu.HBM)
            for array in (
                lengths,
                queries,
                new_keys,
                new_values,
                residual,
                norm_gain.reshape(heads, HD),
                cache_keys,
                cache_values,
                w_gate.T,
                w_down.T,
            )
        ),
    )


def shards(n_g, n_t, *arrays):
    queries, cache_keys = arrays[0], arrays[1]
    rows, steps, features = queries.shape
    heads = features // HD
    kv_heads = cache_keys.shape[2] // HD
    even = (
        n_g == 2 * n_t
        and n_t % 2 == 0
        and heads % n_g == 0
        and n_g % kv_heads == 0
        and steps * (heads // n_g) == 8
        and rows % 2 == 0
        and rows * steps == 8
    )
    if even:
        return moved_activations(n_g, n_t, *arrays)
    return gathered_weights(*arrays)


def solution(mesh):
    return jax.shard_map(
        functools.partial(shards, mesh.shape["grp"], mesh.shape["tp"]),
        mesh=mesh,
        in_specs=(
            P("grp", None, None),
            P("grp", "tp", None),
            P("grp", "tp", None),
            P("grp", None, None),
            P("grp", None, None),
            P("grp"),
            P("grp", None, None),
            P(),
            P("grp", "tp"),
            P("grp", "tp"),
        ),
        out_specs=P("grp", None, None),
        check_vma=False,
    )
```

```python
import functools

import jax
import jax.numpy as jnp
from jax import lax
from jax.experimental import pallas as pl
from jax.experimental.pallas import tpu as pltpu
from jax.sharding import PartitionSpec as P

HD = 128
KVH = 4


masked_score = -1e30


def merged_2(shard, axis, join):
    gathered = jax.tree.map(
        lambda a, kind: lax.all_gather(a.astype(kind), axis),
        shard,
        jax.tree.map(lambda a: jnp.bfloat16 if a.dtype == jnp.float32 else a.dtype, shard),
    )

    def take(source):
        return jax.tree.map(
            lambda a, own: lax.dynamic_index_in_dim(a, source, 0, False).astype(own.dtype),
            gathered,
            shard,
        )

    return lax.fori_loop(
        1, lax.axis_size(axis), lambda source, state: join(state, take(source)), take(0)
    )


def combine_parts(earlier, later):
    first_max, first_total, first_accum = earlier
    second_max, second_total, second_accum = later
    joint_max = jnp.maximum(first_max, second_max)
    first_factor = jnp.exp(first_max - joint_max)
    second_factor = jnp.exp(second_max - joint_max)
    joint_total = first_total * first_factor + second_total * second_factor
    joint_accum = first_accum * first_factor[..., None] + second_accum * second_factor[..., None]
    return (joint_max, joint_total, joint_accum)


def partial_softmax(scores, visible, value_heads, formula):
    scores = jnp.where(visible, scores, masked_score)
    highest = jnp.max(scores, axis=-1)
    weights = jnp.where(visible, jnp.exp(scores - highest[..., None]), 0.0)
    totals = jnp.sum(weights, axis=-1)
    accum = jnp.einsum(
        formula, weights.astype(jnp.bfloat16), value_heads, preferred_element_type=jnp.float32
    )
    return (highest, totals, accum)


def gathered_weights(
    queries,
    cache_keys,
    cache_values,
    new_keys,
    new_values,
    lengths,
    residual,
    norm_gain,
    w_gate,
    w_down,
):
    row_count, step_count, features = queries.shape
    positions = cache_keys.shape[1]
    per_group = features // (KVH * HD)
    inv_root = HD ** (-0.5)
    query_heads = queries.reshape(row_count, step_count, KVH, per_group, HD)
    key_heads = cache_keys.reshape(row_count, positions, KVH, HD)
    value_heads = cache_values.reshape(row_count, positions, KVH, HD)
    cached_scores = (
        jnp.einsum("rsjgd,rcjd->rsjgc", query_heads, key_heads, preferred_element_type=jnp.float32)
        * inv_root
    )
    offset = lax.axis_index("tp") * positions
    places = offset + lax.broadcasted_iota(jnp.int32, (row_count, positions), 1)
    visible = (places < lengths[:, None])[:, None, None, None, :]
    local_part = partial_softmax(cached_scores, visible, value_heads, "rsjgc,rcjd->rsjgd")
    merged = merged_2(local_part, "tp", combine_parts)
    fresh_key_heads = new_keys.reshape(row_count, step_count, KVH, HD)
    fresh_value_heads = new_values.reshape(row_count, step_count, KVH, HD)
    fresh_scores = (
        jnp.einsum(
            "rsjgd,rtjd->rsjgt", query_heads, fresh_key_heads, preferred_element_type=jnp.float32
        )
        * inv_root
    )
    causal = lax.broadcasted_iota(jnp.int32, (step_count, step_count), 0) >= lax.broadcasted_iota(
        jnp.int32, (step_count, step_count), 1
    )
    causal = causal[None, :, None, None, :]
    fresh_part = partial_softmax(fresh_scores, causal, fresh_value_heads, "rsjgt,rtjd->rsjgd")
    joint_max, joint_total, joint_accum = combine_parts(merged, fresh_part)
    context = (joint_accum / joint_total[..., None]).reshape(row_count, step_count, features)
    summed = residual.astype(jnp.float32) + context
    mean_square = jnp.mean(summed * summed, axis=-1, keepdims=True)
    normed = (summed * lax.rsqrt(mean_square + 1e-05) * norm_gain).astype(jnp.bfloat16)
    flat = normed.reshape(row_count * step_count, features)
    gate_policy, down_policy = (
        lax.all_gather(w_gate.astype(jnp.bfloat16), "grp", axis=0, tiled=True),
        lax.all_gather(w_down.astype(jnp.bfloat16), "grp", axis=0, tiled=True),
    )
    gate = jnp.dot(flat, gate_policy, preferred_element_type=jnp.float32)
    hidden = jax.nn.silu(gate).astype(jnp.bfloat16)
    partial_sum = lax.dot_general(
        hidden, down_policy, (((1,), (1,)), ((), ())), preferred_element_type=jnp.float32
    )
    mlp = lax.psum(partial_sum.astype(jnp.bfloat16), "tp").astype(jnp.float32)
    return (summed + mlp.reshape(row_count, step_count, features)).astype(jnp.bfloat16)


MESH = pl.DeviceIdType.MESH
BF16, F32 = jnp.bfloat16, jnp.float32


def layer_kernel(
    n_g,
    n_t,
    lengths_hbm,
    q_hbm,
    nk_hbm,
    nv_hbm,
    res_hbm,
    gain_hbm,
    ck_hbm,
    cv_hbm,
    wg_hbm,
    wd_hbm,
    out_ref,
    lengths_ref,
    q_in,
    nk_in,
    nv_in,
    res_in,
    gain,
    ck,
    cv,
    wg32,
    wd32,
    wg,
    wd,
    q_rows,
    res_rows,
    nk_rows,
    nv_rows,
    send_o,
    recv_o,
    send_x,
    recv_x,
    x_rows,
    x_flat,
    send_g,
    recv_g,
    send_h,
    recv_h,
    send_m,
    recv_m,
    send_f,
    load_sem,
    o_send_sem,
    o_recv_sem,
    m_send_sem,
    m_recv_sem,
    g_send_sem,
    g_recv_sem,
    h_send_sem,
    h_recv_sem,
    x_send_sem,
    x_recv_sem,
    f_send_sem,
    f_recv_sem,
):
    g, t = lax.axis_index("grp"), lax.axis_index("tp")
    rows, positions = ck.shape[0], ck.shape[1]
    steps = nk_in.shape[1]
    heads = gain.shape[0]
    units, depth = wg32.shape
    per_key = heads // KVH
    per_col = heads // n_g
    halves = per_key // per_col
    height = steps * per_col
    inv_root = HD ** (-0.5)
    group_rows = rows * steps
    half_t = n_t // 2

    peer_g = [g] + [lax.rem(g + k, n_g) for k in range(1, n_g)]
    peer_t = [t] + [lax.rem(t + k, n_t) for k in range(1, n_t)]
    far_first = sorted(range(n_t), key=lambda k: (k == 0, abs(k - half_t)))

    barrier = pltpu.get_barrier_semaphore()
    for peer in [(i, t) for i in peer_g[1:]] + [(g, k) for k in peer_t[1:]]:
        pl.semaphore_signal(barrier, inc=1, device_id=peer, device_id_type=MESH)

    loads = [
        pltpu.make_async_copy(source, target, load_sem.at[i])
        for i, (source, target) in enumerate(
            (
                (q_hbm, q_in),
                (lengths_hbm, lengths_ref),
                (ck_hbm, ck),
                (cv_hbm, cv),
                (nk_hbm, nk_in),
                (nv_hbm, nv_in),
                (res_hbm, res_in),
                (gain_hbm, gain),
                (wg_hbm, wg32),
                (wd_hbm, wd32),
            )
        )
    ]
    for load in loads:
        load.start()

    def blocks_of(at):
        first = (at % 2) * n_t + at // 2
        return first, first + half_t

    mine = (lax.rem(t, 2) * n_t + t // 2, lax.rem(t, 2) * n_t + t // 2 + half_t)

    def by_block(source, target):
        flat = jnp.concatenate([source[r].astype(F32) for r in range(rows)], axis=0)
        for h in range(heads):
            target[h // per_col, pl.ds(h % per_col, group_rows, stride=per_col), :] = flat[
                :, h * HD : (h + 1) * HD
            ]

    loads[0].wait()
    by_block(q_in, q_rows)
    loads[1].wait()
    loads[2].wait()
    lane_place = t * positions + lax.broadcasted_iota(jnp.int32, (halves * height, positions), 1)
    pieces, shown = [], []
    tall = halves * height
    blank = jnp.zeros((tall, HD), F32)
    for r in range(rows):
        visible = (lane_place < lengths_ref[r]).astype(F32)
        query = []
        for j in range(KVH):
            own = jnp.concatenate(
                [
                    q_rows[j * halves + i, r * height : (r + 1) * height]
                    for i in range(halves)
                ],
                axis=0,
            )
            query.append(jnp.concatenate([blank] * j + [own] + [blank] * (KVH - 1 - j), axis=1))
            shown.append(visible)
        pieces.append(
            lax.dot_general(
                jnp.concatenate(query, axis=0).astype(BF16),
                ck[r],
                (((1,), (1,)), ((), ())),
                preferred_element_type=F32,
            )
        )
    shown = jnp.concatenate(shown, axis=0) > 0.0
    scores = jnp.where(shown, jnp.concatenate(pieces, axis=0) * inv_root, masked_score)
    highest = jnp.max(scores, axis=-1, keepdims=True)
    weights = jnp.where(shown, jnp.exp(scores - highest), 0.0)
    total = jnp.sum(weights, axis=-1, keepdims=True)
    weights = weights.astype(BF16)
    loads[3].wait()
    accum = []
    for r in range(rows):
        wide = jnp.dot(
            weights[r * KVH * tall : (r + 1) * KVH * tall], cv[r], preferred_element_type=F32
        )
        for j in range(KVH):
            accum.append(wide[j * tall : (j + 1) * tall, j * HD : (j + 1) * HD])
    some = total > 0.0
    safe = jnp.where(some, total, 1.0)
    means = jnp.concatenate(accum, axis=0) / safe
    logs = jnp.where(some, highest + jnp.log(safe), masked_score)

    def of_owner(array, at, i):
        b = blocks_of(at)[i]
        starts = [
            (r * KVH + b // halves) * tall + (b % halves) * height for r in range(rows)
        ]
        return jnp.concatenate([array[at : at + height] for at in starts], axis=0)

    block_rows = rows * height
    off_lane = lax.broadcasted_iota(jnp.int32, (block_rows, HD), 1) - lax.broadcasted_iota(
        jnp.int32, (block_rows, HD), 0
    )
    diagonal = [off_lane == i * block_rows for i in range(2)]
    place = lax.broadcasted_iota(jnp.int32, (send_o.shape[1] - 2 * block_rows, HD), 0)

    log_rows = place.shape[0]
    spans = [(0, block_rows + log_rows), (block_rows + log_rows, block_rows)]

    def fill(at):
        lanes = sum(
            jnp.sum(jnp.where(diagonal[i], of_owner(logs, at, i), 0.0), axis=0, keepdims=True)
            for i in range(2)
        )
        high = lanes.astype(BF16).astype(F32)
        middle = (lanes - high).astype(BF16).astype(F32)
        low = lanes - high - middle
        terms = jnp.where(place == 0, high, jnp.where(place == 1, middle, low))
        send_o[at] = jnp.concatenate(
            [of_owner(means, at, 0), terms, of_owner(means, at, 1)], axis=0
        ).astype(BF16)

    def mean_copy(k, i):
        return pltpu.make_async_remote_copy(
            src_ref=send_o.at[peer_t[k]],
            dst_ref=recv_o.at[t],
            send_sem=o_send_sem.at[i * n_t + k],
            recv_sem=o_recv_sem.at[i * n_t + k],
            device_id=(g, peer_t[k]),
            device_id_type=MESH,
        )

    def along_tp(k, i, source, target, send_sem, recv_sem):
        return pltpu.make_async_remote_copy(
            src_ref=source.at[i, peer_t[k]],
            dst_ref=target.at[i, t],
            send_sem=send_sem.at[i * n_t + k],
            recv_sem=recv_sem.at[i * n_t + k],
            device_id=(g, peer_t[k]),
            device_id_type=MESH,
        )

    for at in range(n_t):
        fill(at)
    pl.semaphore_wait(barrier, n_g + n_t - 2)
    row_copies = [[mean_copy(k, 0) for k in far_first[:-1]], []]
    for copy in row_copies[0] + row_copies[1]:
        copy.start()
    recv_o[t] = send_o[t]

    for load in loads[4:8]:
        load.wait()
    by_block(res_in, res_rows)
    for source, target in ((nk_in, nk_rows), (nv_in, nv_rows)):
        flat = jnp.concatenate([source[r].astype(F32) for r in range(rows)], axis=0)
        for j in range(KVH):
            target[j] = flat[:, j * HD : (j + 1) * HD]

    def new_tokens(tokens, at, b):
        held = tokens[b // halves]
        return jnp.concatenate(
            [
                jnp.broadcast_to(held[r * steps + at : r * steps + at + 1], (height, HD))
                for r in range(rows)
            ],
            axis=0,
        )

    step_of = lax.broadcasted_iota(jnp.int32, (block_rows, 1), 0) & (height - 1)
    seen = [step_of >= at * per_col for at in range(steps)]
    fresh = [
        [
            jnp.where(
                seen[at],
                jnp.sum(q_rows[b] * new_tokens(nk_rows, at, b), axis=-1, keepdims=True)
                * inv_root,
                masked_score,
            )
            for at in range(steps)
        ]
        for b in mine
    ]
    new_held = [[new_tokens(nv_rows, at, b) for at in range(steps)] for b in mine]
    loads[8].wait()
    spare = jnp.zeros((wg.shape[0] - units, depth), F32)
    wg[...] = jnp.concatenate([wg32[...], spare], axis=0).astype(BF16)

    def finish_context(i):
        logs = []
        for at in range(n_t):
            terms = recv_o[at, block_rows : block_rows + log_rows].astype(F32)
            lanes = terms[0:1] + terms[1:2] + terms[2:3]
            logs.append(jnp.sum(jnp.where(diagonal[i], lanes, 0.0), axis=-1, keepdims=True))
        joint = functools.reduce(jnp.maximum, logs + fresh[i])
        total, accum = 0.0, 0.0
        for at in range(n_t):
            weight = jnp.exp(logs[at] - joint)
            total = total + weight
            held = recv_o[at, i * spans[1][0] : i * spans[1][0] + block_rows]
            accum = accum + weight * held.astype(F32)
        for at in range(steps):
            weight = jnp.where(seen[at], jnp.exp(fresh[i][at] - joint), 0.0)
            total = total + weight
            accum = accum + weight.astype(BF16).astype(F32) * new_held[i][at]
        send_x[i] = (res_rows[mine[i]] + accum / total).astype(BF16)

    class Spread:
        def __init__(self, source, target, send_sem, recv_sem):
            self.refs = source, target, send_sem, recv_sem

        def each(self, action, parts):
            source, target, send_sem, recv_sem = self.refs
            for i in parts:
                for k in far_first:
                    copy = pltpu.make_async_remote_copy(
                        src_ref=source.at[i],
                        dst_ref=target(g),
                        send_sem=send_sem.at[i * n_t + k],
                        recv_sem=recv_sem.at[g],
                        device_id=(mine[i], peer_t[k]),
                        device_id_type=MESH,
                    )
                    if k:
                        action(copy)
                    else:
                        pl.when(mine[i] != g)(functools.partial(action, copy))

        def start(self, i):
            self.each(lambda copy: copy.start(), (i,))
            source, target, _, recv_sem = self.refs
            here = pltpu.make_async_copy(source.at[i], target(g), recv_sem.at[g])
            pl.when(mine[i] == g)(here.start)

        def wait_send(self):
            self.each(lambda copy: copy.wait_send(), range(2))

        def wait_recv(self, parts):
            source, target, _, recv_sem = self.refs
            for i in parts:
                pltpu.make_async_copy(source.at[0], target(i), recv_sem.at[i]).wait()

    x_spread = Spread(send_x, lambda i: recv_x.at[i], x_send_sem, x_recv_sem)
    for i in range(2):
        for copy in row_copies[i]:
            copy.wait_recv()
        finish_context(i)
        x_spread.start(i)

    parts = [[blocks_of(at)[i] for at in range(n_t)] for i in range(2)]
    all_rows = n_g * group_rows
    gains = [gain[pl.ds(g * per_col + c, 1)] for c in range(per_col)]

    def part_gate():
        x_spread.wait_recv(range(n_g))
        x_rows[...] = recv_x[...].astype(F32).reshape(x_rows.shape)
        columns = [x_rows[pl.ds(c, all_rows, stride=per_col), :] for c in range(per_col)]
        squares = jnp.sum(
            functools.reduce(jnp.add, [c * c for c in columns]), axis=-1, keepdims=True
        )
        scaled = jnp.concatenate([c * by for c, by in zip(columns, gains)], axis=1).astype(BF16)
        gate = lax.dot_general(
            scaled, wg[...], (((1,), (1,)), ((), ())), preferred_element_type=F32
        )
        spare_lane = lax.broadcasted_iota(jnp.int32, gate.shape, 1) >= units
        gate = jnp.where(spare_lane, squares, gate)
        for b in range(n_g):
            send_g[b] = gate[b * group_rows : (b + 1) * group_rows].astype(BF16)
        return columns

    def along_grp(k, source, target, send_sem, recv_sem):
        return pltpu.make_async_remote_copy(
            src_ref=source,
            dst_ref=target.at[g],
            send_sem=send_sem.at[k - 1],
            recv_sem=recv_sem.at[k - 1],
            device_id=(peer_g[k], t),
            device_id_type=MESH,
        )

    gate_copies = [
        along_grp(k, send_g.at[peer_g[k]], recv_g, g_send_sem, g_recv_sem) for k in range(1, n_g)
    ]
    columns = part_gate()
    for copy in gate_copies:
        copy.start()
    x_flat[...] = jnp.concatenate(columns, axis=1).reshape(x_flat.shape)
    recv_g[g] = send_g[g]
    loads[9].wait()
    wd[...] = jnp.concatenate([wd32[...], spare], axis=0).astype(BF16)
    for copy in gate_copies:
        copy.wait_recv()
    whole = functools.reduce(jnp.add, [recv_g[i].astype(F32) for i in range(n_g)])
    square = whole[:, units : units + 1]
    whole = whole * lax.rsqrt(square / (heads * HD) + 1e-05)
    own_hidden = (whole / (1.0 + jnp.exp(-whole))).astype(BF16)

    send_h[...] = own_hidden
    hidden_copies = [
        pltpu.make_async_remote_copy(
            src_ref=send_h,
            dst_ref=recv_h.at[g],
            send_sem=h_send_sem.at[k],
            recv_sem=h_recv_sem.at[g],
            device_id=(peer_g[k], t),
            device_id_type=MESH,
        )
        for k in range(1, n_g)
    ]
    for copy in hidden_copies:
        copy.start()
    pltpu.make_async_copy(send_h, recv_h.at[g], h_recv_sem.at[g]).start()

    mlp_copies = [
        [along_tp(k, i, send_m, recv_m, m_send_sem, m_recv_sem) for k in far_first[:-1]]
        for i in range(2)
    ]
    for i in range(2):
        for b in parts[i]:
            pltpu.make_async_copy(send_h, recv_h.at[b], h_recv_sem.at[b]).wait()
        hidden = jnp.concatenate([recv_h[b].astype(F32) for b in parts[i]], axis=0).astype(BF16)
        mlp = jnp.dot(hidden, wd[...], preferred_element_type=F32)
        for at in range(n_t):
            send_m[i, at] = mlp[at * group_rows : (at + 1) * group_rows].astype(BF16)
        for copy in mlp_copies[i]:
            copy.start()
        recv_m[i, t] = send_m[i, t]

    def out_columns(i):
        return out_ref.at[:, :, pl.ds(pl.multiple_of(i * depth, depth), depth)]

    f_spread = Spread(send_f, out_columns, f_send_sem, f_recv_sem)
    for i in range(2):
        for copy in mlp_copies[i]:
            copy.wait_recv()
        done = functools.reduce(jnp.add, [recv_m[i, at].astype(F32) for at in range(n_t)])
        done = (x_flat[mine[i]] + done).astype(BF16)
        for r in range(rows):
            send_f[i, r] = done[r * steps : (r + 1) * steps]
        f_spread.start(i)
    for copy in row_copies[0] + row_copies[1] + gate_copies + hidden_copies:
        copy.wait_send()
    for copy in mlp_copies[0] + mlp_copies[1]:
        copy.wait_send()
    x_spread.wait_send()
    f_spread.wait_recv(range(n_g))
    f_spread.wait_send()


def moved_activations(
    n_g,
    n_t,
    queries,
    cache_keys,
    cache_values,
    new_keys,
    new_values,
    lengths,
    residual,
    norm_gain,
    w_gate,
    w_down,
):
    rows, steps, features = queries.shape
    positions, kv_width = cache_keys.shape[1:]
    depth, units = w_gate.shape
    heads = features // HD
    per_col = heads // n_g
    height = steps * per_col
    group_rows = rows * steps
    wide = (units // HD + 1) * HD
    hbm = pl.BlockSpec(memory_space=pltpu.HBM)
    dma = pltpu.SemaphoreType.DMA
    return pl.pallas_call(
        functools.partial(layer_kernel, n_g, n_t),
        out_shape=pltpu.VMEM(queries.shape, BF16),
        in_specs=[hbm] * 10,
        out_specs=pl.BlockSpec(memory_space=pltpu.VMEM),
        scratch_shapes=[
            pltpu.SMEM(lengths.shape, jnp.int32),
            pltpu.VMEM(queries.shape, BF16),
            pltpu.VMEM(new_keys.shape, BF16),
            pltpu.VMEM(new_values.shape, BF16),
            pltpu.VMEM(residual.shape, BF16),
            pltpu.VMEM((heads, HD), F32),
            pltpu.VMEM(cache_keys.shape, BF16),
            pltpu.VMEM(cache_values.shape, BF16),
            pltpu.VMEM((units, depth), F32),
            pltpu.VMEM((units, depth), F32),
            pltpu.VMEM((wide, depth), BF16),
            pltpu.VMEM((wide, depth), BF16),
            pltpu.VMEM((n_g, rows * height, HD), F32),
            pltpu.VMEM((n_g, rows * height, HD), F32),
            pltpu.VMEM((KVH, group_rows, HD), F32),
            pltpu.VMEM((KVH, group_rows, HD), F32),
            pltpu.VMEM((n_t, 2 * rows * height + 16, HD), BF16),
            pltpu.VMEM((n_t, 2 * rows * height + 16, HD), BF16),
            pltpu.VMEM((2, rows * height, HD), BF16),
            pltpu.VMEM((n_g, rows * height, HD), BF16),
            pltpu.VMEM((n_g * rows * height, HD), F32),
            pltpu.VMEM((n_g, group_rows, depth), F32),
            pltpu.VMEM((n_g, group_rows, wide), BF16),
            pltpu.VMEM((n_g, group_rows, wide), BF16),
            pltpu.VMEM((group_rows, wide), BF16),
            pltpu.VMEM((n_g, group_rows, wide), BF16),
            pltpu.VMEM((2, n_t, group_rows, depth), BF16),
            pltpu.VMEM((2, n_t, group_rows, depth), BF16),
            pltpu.VMEM((2, rows, steps, depth), BF16),
            dma((10,)),
        ]
        + [dma((2 * n_t,))] * 4
        + [dma((n_g,))] * 8,
        compiler_params=pltpu.CompilerParams(
            collective_id=0, has_side_effects=True, vmem_limit_bytes=40 * 1024 * 1024
        ),
    )(
        *(
            pltpu.with_memory_space_constraint(array, pltpu.HBM)
            for array in (
                lengths,
                queries,
                new_keys,
                new_values,
                residual,
                norm_gain.reshape(heads, HD),
                cache_keys,
                cache_values,
                w_gate.T,
                w_down.T,
            )
        ),
    )


def shards(n_g, n_t, *arrays):
    queries, cache_keys = arrays[0], arrays[1]
    rows, steps, features = queries.shape
    heads = features // HD
    kv_heads = cache_keys.shape[2] // HD
    even = (
        n_g == 2 * n_t
        and n_t % 2 == 0
        and heads % n_g == 0
        and n_g % kv_heads == 0
        and steps * (heads // n_g) == 8
        and rows % 2 == 0
        and rows * steps == 8
    )
    if even:
        return moved_activations(n_g, n_t, *arrays)
    return gathered_weights(*arrays)


def solution(mesh):
    return jax.shard_map(
        functools.partial(shards, mesh.shape["grp"], mesh.shape["tp"]),
        mesh=mesh,
        in_specs=(
            P("grp", None, None),
            P("grp", "tp", None),
            P("grp", "tp", None),
            P("grp", None, None),
            P("grp", None, None),
            P("grp"),
            P("grp", None, None),
            P(),
            P("grp", "tp"),
            P("grp", "tp"),
        ),
        out_specs=P("grp", None, None),
        check_vma=False,
    )
```
